1024 devices in a mesh: ctx: 8 (over z_hi, core), tp: 8 (over x), dp: 16 (over y, z_lo).
Axes of the slice: x: 8, y: 8, z: 8 (z_hi: 4, z_lo: 2; z = z_hi * 2 + z_lo), core: 2. Of those that a mesh axis runs over, the one named last changes fastest.
Arguments:
- grad_out: bfloat16 [16, 1024, 4096], P('dp', 'ctx'), may hold values from -6 to 6
- expert_input: bfloat16 [8, 16, 8, 19, 4096], P('ctx', 'dp'), may hold values from -6 to 6
- expert_ids: int32 [16, 1024], P('dp', 'ctx'), may hold values from 0 to 7, as said below
- slots: int32 [16, 1024], P('dp', 'ctx'), may hold values from 0 to 18, as said below
- w_gate: bfloat16 [8, 4096, 2048], P('ctx', None, 'tp'), may hold values from -0.09375 to 0.09375
- w_up: bfloat16 [8, 4096, 2048], P('ctx', None, 'tp'), may hold values from -0.09375 to 0.09375
- w_down: bfloat16 [8, 2048, 4096], P('ctx', 'tp'), may hold values from -0.125 to 0.125
Outputs:
- grad_input: bfloat16 [16, 1024, 4096], P('dp', 'ctx', 'tp')
- grad_gate: float32 [8, 4096, 2048], P('ctx', 'dp', 'tp')
- grad_up: float32 [8, 4096, 2048], P('ctx', 'dp', 'tp')
The draws below stay inside these ranges and needn't reach their ends.
Inputs may be any that keep to these rules, and one draw needn't show every extreme that they name: `expert_ids`: among the 128 tokens of one source of a group, no expert is named more than 19 times, and in every group one expert is named exactly 19 times by every source. Tokens of one source of a group that name the same expert have different slots.
All inputs are finite; a program needn't handle non-finite values.
Results may differ from the reference program's by a relative error of at most 0.022.
Values may be sent and summed in bfloat16 or wider, within the bound.
A program may use at most 64 MiB of HBM per device.

```python
import jax
import jax.numpy as jnp
from jax import lax

D = 4096
FF = 2048
TOK_DEV = 128
EXPERTS = 8
CAP = 19
GROUPS = 16
GROUP_TOK = 1024
N_CTX = 8
N_TP = 8
N_DP = 16


def routing_positions(key):
    hot_experts = jax.random.randint(jax.random.fold_in(key, 101), (GROUPS,), 0, EXPERTS)

    def one_block(block_number):
        block_key = jax.random.fold_in(key, 1000 + block_number)
        rest_key, order_key = jax.random.split(block_key)
        hot_expert = hot_experts[block_number // N_CTX]
        chosen = jax.random.permutation(rest_key, (EXPERTS - 1) * CAP)[:TOK_DEV - CAP].astype(jnp.int32)
        other_expert = chosen // CAP
        other_expert = other_expert + (other_expert >= hot_expert).astype(jnp.int32)
        positions = jnp.concatenate([hot_expert * CAP + jnp.arange(CAP, dtype=jnp.int32), other_expert * CAP + chosen % CAP])
        return jax.random.permutation(order_key, positions)
    table = jax.vmap(one_block)(jnp.arange(GROUPS * N_CTX, dtype=jnp.int32))
    return table.reshape(GROUPS, GROUP_TOK).astype(jnp.int32)


def draw_expert_ids(key, part):
    return routing_positions(key) // CAP


def draw_slots(key, part):
    return routing_positions(key) % CAP


def spiked(values, own_key, source, target, shards_of, factor):
    owner, partner = [(jnp.arange(values.shape[position]) // (values.shape[position] // shards_of)).reshape([-1 if axis == position else 1 for axis in range(values.ndim)]) for position in (source, target)]
    chosen = jax.random.permutation(own_key, shards_of)[partner]
    strong = (owner == chosen) | (owner == (partner + shards_of // 2) % shards_of)
    return jnp.where(strong, factor * values, values)


def block_scale(stream_key, extent, pieces, smallest, top_value):
    def one(position, shards_of):
        steps = jax.random.uniform(jax.random.fold_in(jax.random.fold_in(stream_key, 6), position), (shards_of,), jnp.float32, smallest / len(pieces), top_value / len(pieces))
        return jnp.repeat(jnp.exp(steps), extent[position] // shards_of).reshape((-1,) + (1,) * (len(extent) - position - 1))

    gain = one(*pieces[0])
    for cut in pieces[1:]:
        gain = gain * one(*cut)
    return gain


def scatter_about(rng, dims, scale, reach, shards=(), held_as=jnp.bfloat16):
    gain = block_scale(rng, dims, shards, -0.22, 0.18) if shards else 1.0
    array = jax.random.normal(rng, dims, jnp.float32) * scale * gain
    return jnp.minimum(jnp.maximum(array, -reach), reach).astype(held_as)


def noise_with(rng, extent, spread, limit, cuts, heavy, kind=jnp.bfloat16):
    array = spread * jax.random.normal(rng, extent, jnp.float32)
    if cuts:
        array = array * block_scale(rng, extent, cuts, -0.22, 0.18)
    return jnp.clip(spiked(array, jax.random.fold_in(rng, 3), *heavy), -limit, limit).astype(kind)


def setup_inputs(seed: int = 0) -> dict:
    arg_keys = jax.random.split(jax.random.key(seed), 8)
    grad_out = scatter_about(arg_keys[0], (GROUPS, GROUP_TOK, D), 1.0, 6.0, ((0, 16), (1, 8)))
    expert_input = noise_with(arg_keys[1], (EXPERTS, GROUPS, N_CTX, CAP, D), 1.0, 6.0, ((0, 8), (1, 16)), (1, 4, 16, 2.0))
    expert_ids = draw_expert_ids(jax.random.fold_in(arg_keys[7], 71), 0)
    slots = draw_slots(jax.random.fold_in(arg_keys[7], 71), 0)
    w_gate = scatter_about(arg_keys[4], (EXPERTS, D, FF), D ** -0.5, 0.09375, ((0, 8), (2, 8)))
    w_up = scatter_about(arg_keys[5], (EXPERTS, D, FF), D ** -0.5, 0.09375, ((0, 8), (2, 8)))
    w_down = scatter_about(arg_keys[6], (EXPERTS, FF, D), FF ** -0.5, 0.125, ((0, 8), (1, 8)))
    return dict(grad_out=grad_out, expert_input=expert_input, expert_ids=expert_ids, slots=slots, w_gate=w_gate, w_up=w_up, w_down=w_down)


def rounded(values):
    return lax.optimization_barrier(values.astype(jnp.bfloat16)).astype(jnp.float32)


def reference(grad_out, expert_input, expert_ids, slots, w_gate, w_up, w_down):
    rows_exp = N_CTX * CAP
    block_ff = FF // N_TP
    contract_last = (((1,), (1,)), ((), ()))
    contract_first = (((0,), (0,)), ((), ()))
    source = (jnp.arange(GROUP_TOK, dtype=jnp.int32) // TOK_DEV)[None, :]
    flat_index = (expert_ids * rows_exp + source * CAP + slots).astype(jnp.int32)
    group_index = jnp.broadcast_to(jnp.arange(GROUPS, dtype=jnp.int32)[:, None], flat_index.shape)
    routed = jnp.zeros((GROUPS, EXPERTS * rows_exp, D), jnp.bfloat16).at[group_index, flat_index].set(grad_out)
    routed = routed.reshape(GROUPS, EXPERTS, rows_exp, D).transpose(1, 0, 2, 3)
    inputs_all = expert_input.reshape(EXPERTS, GROUPS, rows_exp, D)

    def per_expert(operands):
        saved, incoming, gate_weights, up_weights, down_weights = operands
        saved_flat = saved.reshape(GROUPS * rows_exp, D)
        incoming_flat = incoming.reshape(GROUPS * rows_exp, D)
        gate = jnp.dot(saved_flat, gate_weights, preferred_element_type=jnp.float32)
        upward = jnp.dot(saved_flat, up_weights, preferred_element_type=jnp.float32)
        grad_hidden = lax.dot_general(incoming_flat, down_weights, contract_last, preferred_element_type=jnp.float32)
        sigmoid_gate = jax.nn.sigmoid(gate)
        grad_gate_pre = (grad_hidden * upward * sigmoid_gate * (1.0 + gate * (1.0 - sigmoid_gate))).astype(jnp.bfloat16)
        grad_up_pre = (grad_hidden * gate * sigmoid_gate).astype(jnp.bfloat16)

        def add_block(blocknum, carried):
            offset = blocknum * block_ff
            term = lax.dot_general(lax.dynamic_slice_in_dim(grad_gate_pre, offset, block_ff, 1),
                                   lax.dynamic_slice_in_dim(gate_weights, offset, block_ff, 1),
                                   contract_last, preferred_element_type=jnp.float32)
            term = term + lax.dot_general(lax.dynamic_slice_in_dim(grad_up_pre, offset, block_ff, 1),
                                          lax.dynamic_slice_in_dim(up_weights, offset, block_ff, 1),
                                          contract_last, preferred_element_type=jnp.float32)
            return carried + rounded(term)

        slot_grad = lax.fori_loop(0, N_TP, add_block, jnp.zeros((GROUPS * rows_exp, D), jnp.float32))
        slot_grad = slot_grad.astype(jnp.bfloat16)
        hidden_cat = jnp.concatenate([grad_gate_pre, grad_up_pre], axis=1)

        def add_group(groupnum, carried):
            offset = groupnum * rows_exp
            group_part = lax.dot_general(lax.dynamic_slice_in_dim(saved_flat, offset, rows_exp, 0),
                                         lax.dynamic_slice_in_dim(hidden_cat, offset, rows_exp, 0),
                                         contract_first, preferred_element_type=jnp.float32)
            return carried + rounded(group_part)

        weight_grad = lax.fori_loop(0, GROUPS, add_group, jnp.zeros((D, 2 * FF), jnp.float32)) / N_DP
        return slot_grad.reshape(GROUPS, rows_exp, D), weight_grad[:, :FF], weight_grad[:, FF:]

    slot_grad, grad_gate, grad_up = lax.map(per_expert, (inputs_all, routed, w_gate, w_up, w_down))
    slot_grad = slot_grad.transpose(1, 0, 2, 3).reshape(GROUPS, EXPERTS * rows_exp, D)
    grad_input = jnp.take_along_axis(slot_grad, flat_index[:, :, None], axis=1)
    return grad_input, grad_gate, grad_up
```

```python
import jax
import jax.numpy as jnp
from jax import lax
from jax.experimental import pallas as pl
from jax.experimental.pallas import tpu as pltpu
from jax.sharding import PartitionSpec as P

MESH = pl.DeviceIdType.MESH
BF16 = jnp.bfloat16
F32 = jnp.float32

RING = 8
CAP = 19
ROWS = RING * CAP
MAIN = 16
TOK = 128
D = 4096
FEAT = D // RING
H = FEAT // 2
FB = 256
PACK = FEAT + 128


def mm(a, b, ca, cb):
    return lax.dot_general(a, b, (((ca,), (cb,)), ((), ())), preferred_element_type=F32)


def iota(shape, dim):
    return lax.broadcasted_iota(jnp.int32, shape, dim)


def onehot(mask):
    return jnp.where(mask, 1.0, 0.0).astype(BF16)


def kernel(
    ids, slots, tok_hbm, x_hbm, wg_hbm, wu_hbm, wd_hbm,
    gi_out, gg_out, gu_out,
    tok, x, wg, wu, wd, route_out, route_in, routed, xt, pa, part, from_left, from_right, back_out, back_in, w_out, w_in,
    load_sem, xload_sem,
    route_ss, route_rs, xt_ss, xt_rs, tp_ss, tp_rs, dp_ss, dp_rs, rs_ss, rs_rs, back_ss, back_rs, w_ss, w_rs,
):
    e, t, d = lax.axis_index("ctx"), lax.axis_index("tp"), lax.axis_index("dp")
    y, a = d // 2, d % 2

    def ctx(s):
        return {"ctx": (e + s) % RING}

    def tp(s):
        return {"tp": (t + s + RING) % RING}

    def dpy(s):
        return {"dp": ((y + s + RING) % RING) * 2 + a}

    twin = {"dp": y * 2 + 1 - a}
    started = []

    def send(src, dst, ss, rs, dev):
        copy = pltpu.make_async_remote_copy(
            src_ref=src, dst_ref=dst, send_sem=ss, recv_sem=rs, device_id=dev, device_id_type=MESH
        )
        copy.start()
        started.append(copy)
        return copy

    load_tok = pltpu.make_async_copy(
        tok_hbm.at[0, :, pl.ds(pl.multiple_of(t * FEAT, FEAT), FEAT)], tok, load_sem.at[0]
    )
    load_tok.start()
    load_x = [
        pltpu.make_async_copy(x_hbm.at[:, pl.ds(j * H, H)], x.at[j], xload_sem.at[j]) for j in range(2 * RING)
    ]
    for copy in load_x:
        copy.start()
    load_wg = pltpu.make_async_copy(wg_hbm.at[0], wg, load_sem.at[1])
    load_wu = pltpu.make_async_copy(wu_hbm.at[0], wu, load_sem.at[2])
    load_wd = pltpu.make_async_copy(wd_hbm.at[0], wd, load_sem.at[3])
    load_wg.start()
    load_wu.start()
    load_wd.start()

    barrier = pltpu.get_barrier_semaphore()
    peers = [ctx(s) for s in range(1, RING)] + [tp(1), tp(-1)] + [dpy(s) for s in range(1, RING)] + [twin]
    for peer in peers:
        pl.semaphore_signal(barrier, inc=1, device_id=peer, device_id_type=MESH)

    expert, slot = ids[...], slots[...]
    main_row = jnp.where(slot < MAIN, expert * MAIN + slot, -1)
    fold_row = jnp.where(slot < MAIN, -8, expert * MAIN + 4 * (slot - MAIN))
    rows = iota((TOK, TOK), 0)
    to_main = onehot(rows == main_row)
    to_fold = [onehot(rows == fold_row + q) for q in range(4)]
    cols = iota((TOK, TOK), 1)
    main_map = onehot(cols == (rows % RING) * MAIN + rows // RING)
    erow = iota((3 * RING, TOK), 0)
    ecol = iota((3 * RING, TOK), 1)
    fold_map = [onehot(ecol == (erow % RING) * MAIN + 4 * (erow // RING) + q) for q in range(4)]

    load_tok.wait()
    mine = tok[...]
    route_out[:, :, :FEAT] = mm(to_main, mine, 1, 0).astype(BF16).reshape(RING, MAIN, FEAT)
    folded = mm(to_fold[0], mine[:, :128], 1, 0)
    for q in range(1, 4):
        folded = folded + mm(to_fold[q], mine[:, 128 * q:128 * q + 128], 1, 0)
    route_out[:, :, FEAT:] = folded.astype(BF16).reshape(RING, MAIN, 128)
    route_in[e] = route_out[e]

    pl.semaphore_wait(barrier, len(peers))
    route = [None] + [
        send(route_out.at[(e + s) % RING], route_in.at[e], route_ss.at[s], route_rs.at[s], ctx(s))
        for s in range(1, RING)
    ]

    for copy in load_x:
        copy.wait()
    xts = {}
    for s in (1, 7, 2, 6, 3, 5, 4):
        for h in range(2):
            xts[s, h] = send(
                x.at[((y + s) % RING) * 2 + h], xt.at[s, h], xt_ss.at[s, h], xt_rs.at[s, h], dpy(s)
            )
    for h in range(2):
        xt[0, h] = x[y * 2 + h]

    load_wg.wait()
    load_wu.wait()
    gate = mm(x[0], wg[:H, :], 1, 0)
    upward = mm(x[0], wu[:H, :], 1, 0)
    for j in range(1, 2 * RING):
        gate = gate + mm(x[j], wg[j * H:j * H + H, :], 1, 0)
        upward = upward + mm(x[j], wu[j * H:j * H + H, :], 1, 0)
    sig = 1.0 / (1.0 + jnp.exp(-gate))
    up_factor = gate * sig
    gate_factor = upward * sig * (1.0 + gate * (1.0 - sig))

    for s in range(1, RING):
        route[s].wait_recv()
    main_in = route_in[:, :, :FEAT].reshape(TOK, FEAT)
    fold_in = route_in[:, :, FEAT:].reshape(TOK, 128)
    main_part = mm(main_map, main_in, 1, 0).astype(BF16)
    fold_part = [mm(m, fold_in, 1, 0).astype(BF16) for m in fold_map]
    for h in range(2):
        routed[0, h, :TOK, :] = main_part[:, h * H:h * H + H]
        routed[0, h, TOK:, :128] = fold_part[2 * h]
        routed[0, h, TOK:, 128:] = fold_part[2 * h + 1]

    def ring_send(buf, ss, rs, k, h, peer, sign):
        src, dst = (k - 1, k) if sign > 0 else ((RING + 1 - k) % RING, RING - k)
        way = 0 if sign > 0 else 1
        return send(buf.at[src, h], buf.at[dst, h], ss.at[way, k - 1, h], rs.at[way, k - 1, h], peer(sign))

    def ring_begin(buf, ss, rs, peer):
        flight = {}
        for h in range(2):
            for sign in (1, -1):
                flight[sign, 1, h] = ring_send(buf, ss, rs, 1, h, peer, sign)
        return flight

    def ring_step(flight, buf, ss, rs, peer, k, h):
        for sign in (1, -1):
            flight[sign, k, h].wait_recv()
            if k < 3 or h == (0 if sign > 0 else 1):
                flight[sign, k + 1, h] = ring_send(buf, ss, rs, k + 1, h, peer, sign)

    def ring_end(flight):
        flight[1, 4, 0].wait_recv()
        flight[-1, 4, 1].wait_recv()

    flight = ring_begin(routed, tp_ss, tp_rs, tp)
    load_wd.wait()

    def hidden_term(s, h):
        first = ((t - s + RING) % RING) * FEAT + h * H
        return mm(routed[s, h], wd[:, pl.ds(pl.multiple_of(first, H), H)], 1, 1)

    grad_hidden = hidden_term(0, 0) + hidden_term(0, 1)
    for k in range(1, 4):
        for h in range(2):
            ring_step(flight, routed, tp_ss, tp_rs, tp, k, h)
            grad_hidden = grad_hidden + hidden_term(k, h) + hidden_term(RING - k, h)
    ring_end(flight)
    grad_hidden = grad_hidden + hidden_term(4, 0) + hidden_term(4, 1)

    grad_gate_pre = (grad_hidden * gate_factor).astype(BF16)
    grad_up_pre = (grad_hidden * up_factor).astype(BF16)
    pa[0, 0] = grad_gate_pre
    pa[0, 1] = grad_up_pre
    dp_flight = ring_begin(pa, dp_ss, dp_rs, dpy)

    def partial_term(j, h):
        first = pl.ds(pl.multiple_of(((t + j) % RING) * FEAT + h * H, H), H)
        part[j, h] = (mm(grad_gate_pre, wg[first, :], 1, 1) + mm(grad_up_pre, wu[first, :], 1, 1)).astype(BF16)

    rs_flight = {}

    def sum_send(sign, k, h):
        way = 0 if sign > 0 else 1
        slot_ = k if sign > 0 else RING - k
        dst = (from_left if sign > 0 else from_right).at[k - 1, h]
        rs_flight[sign, k, h] = send(
            part.at[slot_, h], dst, rs_ss.at[way, k - 1, h], rs_rs.at[way, k - 1, h], tp(sign)
        )

    def sum_step(sign, k, h):
        rs_flight[sign, k + 1, h].wait_recv()
        slot_ = k if sign > 0 else RING - k
        arrived = (from_left if sign > 0 else from_right)[k, h]
        part[slot_, h] = (part[slot_, h].astype(F32) + arrived.astype(F32)).astype(BF16)
        sum_send(sign, k, h)

    partial_term(4, 0)
    sum_send(1, 4, 0)
    partial_term(4, 1)
    sum_send(-1, 4, 1)
    partial_term(3, 1)
    sum_send(1, 3, 1)
    partial_term(5, 0)
    sum_send(-1, 3, 0)
    partial_term(3, 0)
    partial_term(5, 1)

    ring_step(dp_flight, pa, dp_ss, dp_rs, dpy, 1, 0)
    sum_step(1, 3, 0)
    sum_step(-1, 3, 1)
    for j in (2, 6):
        for h in range(2):
            partial_term(j, h)
    ring_step(dp_flight, pa, dp_ss, dp_rs, dpy, 1, 1)
    sum_step(1, 2, 1)
    sum_step(-1, 2, 0)
    ring_step(dp_flight, pa, dp_ss, dp_rs, dpy, 2, 0)
    sum_step(1, 2, 0)
    sum_step(-1, 2, 1)
    for j in (1, 7, 0):
        for h in range(2):
            partial_term(j, h)
    ring_step(dp_flight, pa, dp_ss, dp_rs, dpy, 2, 1)
    sum_step(1, 1, 1)
    sum_step(-1, 1, 0)
    ring_step(dp_flight, pa, dp_ss, dp_rs, dpy, 3, 0)
    sum_step(1, 1, 0)
    sum_step(-1, 1, 1)
    ring_step(dp_flight, pa, dp_ss, dp_rs, dpy, 3, 1)

    for copy in xts.values():
        copy.wait_recv()
    ring_end(dp_flight)

    def weight_term(half, which):
        total = mm(xt[0, half], pa[0, which], 0, 0)
        for s in range(1, RING):
            total = total + mm(xt[s, half], pa[s, which], 0, 0)
        return total

    w_flight = []
    for which in range(2):
        w_out[which] = weight_term(1 - a, which).astype(BF16)
        w_flight.append(send(w_out.at[which], w_in.at[which], w_ss.at[which], w_rs.at[which], twin))

    for h in (1, 0):
        rs_flight[1, 1, h].wait_recv()
        rs_flight[-1, 1, h].wait_recv()
    slot_grad = [
        (part[0, h].astype(F32) + from_left[0, h].astype(F32) + from_right[0, h].astype(F32)).astype(BF16)
        for h in range(2)
    ]
    for h in range(2):
        back_out[:, :, h * H:h * H + H] = mm(main_map, slot_grad[h][:TOK, :], 0, 0).astype(BF16).reshape(RING, MAIN, H)
    folded = mm(fold_map[0], slot_grad[0][TOK:, :128], 0, 0)
    for q in range(1, 4):
        folded = folded + mm(fold_map[q], slot_grad[q // 2][TOK:, (q % 2) * 128:(q % 2) * 128 + 128], 0, 0)
    back_out[:, :, FEAT:] = folded.astype(BF16).reshape(RING, MAIN, 128)
    back_in[e] = back_out[e]
    back = [
        send(back_out.at[(e + s) % RING], back_in.at[e], back_ss.at[s], back_rs.at[s], ctx(s)) for s in range(1, RING)
    ]

    own = [weight_term(a, which) for which in range(2)]

    for copy in back:
        copy.wait_recv()
    main_in = back_in[:, :, :FEAT].reshape(TOK, FEAT)
    fold_in = back_in[:, :, FEAT:].reshape(TOK, 128)
    token_rows = mm(to_main, main_in, 0, 0)
    for q in range(4):
        piece = slice(128 * q, 128 * q + 128)
        gi_out[0, :, piece] = (token_rows[:, piece] + mm(to_fold[q], fold_in, 0, 0)).astype(BF16)

    for which, out in enumerate((gg_out, gu_out)):
        w_flight[which].wait_recv()
        out[0] = (own[which] + w_in[which].astype(F32)) * (1.0 / 16.0)

    for copy in started:
        copy.wait_send()


def body(grad_out, expert_input, expert_ids, slots, w_gate, w_up, w_down):
    saved = expert_input.transpose(0, 1, 3, 2, 4).reshape(ROWS, D)
    vmem = pl.BlockSpec(memory_space=pltpu.VMEM)
    hbm = pl.BlockSpec(memory_space=pl.ANY)
    dma = pltpu.SemaphoreType.DMA
    piece = (2, ROWS, H)
    return pl.pallas_call(
        kernel,
        out_shape=(
            jax.ShapeDtypeStruct((1, TOK, FEAT), BF16),
            jax.ShapeDtypeStruct((1, 256, FB), F32),
            jax.ShapeDtypeStruct((1, 256, FB), F32),
        ),
        in_specs=[vmem, vmem] + [hbm] * 5,
        out_specs=(vmem, vmem, vmem),
        scratch_shapes=[
            pltpu.VMEM((TOK, FEAT), BF16),
            pltpu.VMEM((2 * RING, ROWS, H), BF16),
            pltpu.VMEM((D, FB), BF16),
            pltpu.VMEM((D, FB), BF16),
            pltpu.VMEM((FB, D), BF16),
            pltpu.VMEM((RING, MAIN, PACK), BF16),
            pltpu.VMEM((RING, MAIN, PACK), BF16),
            pltpu.VMEM((RING,) + piece, BF16),
            pltpu.VMEM((RING,) + piece, BF16),
            pltpu.VMEM((RING,) + piece, BF16),
            pltpu.VMEM((RING,) + piece, BF16),
            pltpu.VMEM((4,) + piece, BF16),
            pltpu.VMEM((4,) + piece, BF16),
            pltpu.VMEM((RING, MAIN, PACK), BF16),
            pltpu.VMEM((RING, MAIN, PACK), BF16),
            pltpu.VMEM((2, 256, FB), BF16),
            pltpu.VMEM((2, 256, FB), BF16),
            dma((4,)),
            dma((2 * RING,)),
            dma((RING,)),
            dma((RING,)),
            dma((RING, 2)),
            dma((RING, 2)),
            dma((2, 4, 2)),
            dma((2, 4, 2)),
            dma((2, 4, 2)),
            dma((2, 4, 2)),
            dma((2, 4, 2)),
            dma((2, 4, 2)),
            dma((RING,)),
            dma((RING,)),
            dma((2,)),
            dma((2,)),
        ],
        compiler_params=pltpu.CompilerParams(
            collective_id=0, has_side_effects=True, vmem_limit_bytes=40 * 1024 * 1024
        ),
        name="expert_backward",
    )(expert_ids, slots, grad_out, saved, w_gate, w_up, w_down)


def solution(mesh):
    return jax.shard_map(
        body,
        mesh=mesh,
        in_specs=(
            P("dp", "ctx", None),
            P("ctx", "dp", None, None, None),
            P("dp", "ctx"),
            P("dp", "ctx"),
            P("ctx", None, "tp"),
            P("ctx", None, "tp"),
            P("ctx", "tp", None),
        ),
        out_specs=(P("dp", "ctx", "tp"), P("ctx", "dp", "tp"), P("ctx", "dp", "tp")),
        check_vma=False,
    )
```

```python
import jax
import jax.numpy as jnp
from jax import lax
from jax.experimental import pallas as pl
from jax.experimental.pallas import tpu as pltpu
from jax.sharding import PartitionSpec as P

MESH = pl.DeviceIdType.MESH
BF16 = jnp.bfloat16
F32 = jnp.float32

RING = 8
CAP = 19
ROWS = RING * CAP
MAIN = 16
TOK = 128
D = 4096
FEAT = D // RING
H = FEAT // 2
FB = 256
PACK = FEAT + 128


def mm(a, b, ca, cb):
    return lax.dot_general(a, b, (((ca,), (cb,)), ((), ())), preferred_element_type=F32)


def iota(shape, dim):
    return lax.broadcasted_iota(jnp.int32, shape, dim)


def onehot(mask):
    return jnp.where(mask, 1.0, 0.0).astype(BF16)


def kernel(
    ids_hbm, slots_hbm, tok_hbm, x_hbm, wg_hbm, wu_hbm, wd_hbm,
    gi_out, gg_out, gu_out,
    ids, slots, tok, x, wg, wu, wd, route_out, route_in, routed, xt, pa, part, from_left, from_right, back_out, back_in, w_out, w_in, acc,
    load_sem, tok_sem, xload_sem,
    route_ss, route_rs, xt_ss, xt_rs, tp_ss, tp_rs, dp_ss, dp_rs, rs_ss, rs_rs, back_ss, back_rs, w_ss, w_rs,
):
    e, t, d = lax.axis_index("ctx"), lax.axis_index("tp"), lax.axis_index("dp")
    y, a = d // 2, d % 2

    def ctx(s):
        return {"ctx": (e + s) % RING}

    def tp(s):
        return {"tp": (t + s + RING) % RING}

    def dpy(s):
        return {"dp": ((y + s + RING) % RING) * 2 + a}

    twin = {"dp": y * 2 + 1 - a}
    started = []

    def send(src, dst, ss, rs, dev):
        copy = pltpu.make_async_remote_copy(
            src_ref=src, dst_ref=dst, send_sem=ss, recv_sem=rs, device_id=dev, device_id_type=MESH
        )
        copy.start()
        started.append(copy)
        return copy

    load_ids = pltpu.make_async_copy(ids_hbm, ids, load_sem.at[4])
    load_slots = pltpu.make_async_copy(slots_hbm, slots, load_sem.at[5])
    load_ids.start()
    load_slots.start()
    load_tok = []
    for r, c, first in ((0, 0, t * 2), (0, 1, t * 2 + 1), (1, 0, (t + 4) % RING * 2), (1, 1, (t + 4) % RING * 2 + 1),
                        (2, 0, (t + 5) % RING * 2 + 1), (2, 1, (t + 3) % RING * 2)):
        load_tok.append(
            pltpu.make_async_copy(
                tok_hbm.at[0, :, pl.ds(pl.multiple_of(first * H, H), H)], tok.at[r, c], tok_sem.at[r, c]
            )
        )
        load_tok[-1].start()
    load_x = [
        pltpu.make_async_copy(x_hbm.at[:, pl.ds(j * H, H)], x.at[j], xload_sem.at[j]) for j in range(2 * RING)
    ]
    for copy in load_x:
        copy.start()
    load_wg = pltpu.make_async_copy(wg_hbm.at[0], wg, load_sem.at[1])
    load_wu = pltpu.make_async_copy(wu_hbm.at[0], wu, load_sem.at[2])
    load_wd = pltpu.make_async_copy(wd_hbm.at[0], wd, load_sem.at[3])
    load_wg.start()
    load_wu.start()
    load_wd.start()

    barrier = pltpu.get_barrier_semaphore()
    peers = [ctx(s) for s in range(1, RING)] + [tp(1), tp(-1)] + [dpy(s) for s in range(1, RING)] + [twin]
    for peer in peers:
        pl.semaphore_signal(barrier, inc=1, device_id=peer, device_id_type=MESH)

    load_ids.wait()
    load_slots.wait()
    expert, slot = ids[...], slots[...]
    main_row = jnp.where(slot < MAIN, expert * MAIN + slot, -1)
    fold_row = jnp.where(slot < MAIN, -8, expert * MAIN + 4 * (slot - MAIN))
    rows = iota((TOK, TOK), 0)
    to_main = onehot(rows == main_row)
    to_fold = [onehot(rows == fold_row + q) for q in range(4)]
    cols = iota((TOK, TOK), 1)
    main_map = onehot(cols == (rows % RING) * MAIN + rows // RING)
    erow = iota((3 * RING, TOK), 0)
    ecol = iota((3 * RING, TOK), 1)
    fold_map = [onehot(ecol == (erow % RING) * MAIN + 4 * (erow // RING) + q) for q in range(4)]

    def pack(r):
        load_tok[2 * r].wait()
        load_tok[2 * r + 1].wait()
        halves = [tok[r, c] for c in range(2)]
        for c in range(2):
            route_out[r, :, :, c * H:c * H + H] = mm(to_main, halves[c], 1, 0).astype(BF16).reshape(RING, MAIN, H)
        folded = mm(to_fold[0], halves[0][:, :128], 1, 0)
        for q in range(1, 4):
            folded = folded + mm(to_fold[q], halves[q // 2][:, (q % 2) * 128:(q % 2) * 128 + 128], 1, 0)
        route_out[r, :, :, FEAT:] = folded.astype(BF16).reshape(RING, MAIN, 128)
        route_in[r, e] = route_out[r, e]

    def route_set(r):
        return [
            send(
                route_out.at[r, (e + s) % RING], route_in.at[r, e], route_ss.at[r, s], route_rs.at[r, s], ctx(s)
            )
            for s in range(1, RING)
        ]

    def unpack(r, places):
        for copy in route[r]:
            copy.wait_recv()
        main_in = route_in[r, :, :, :FEAT].reshape(TOK, FEAT)
        fold_in = route_in[r, :, :, FEAT:].reshape(TOK, 128)
        main_part = mm(main_map, main_in, 1, 0).astype(BF16)
        fold_part = [mm(m, fold_in, 1, 0).astype(BF16) for m in fold_map]
        for c, (s, h) in enumerate(places):
            routed[s, h, :TOK, :] = main_part[:, c * H:c * H + H]
            routed[s, h, TOK:, :128] = fold_part[2 * c]
            routed[s, h, TOK:, 128:] = fold_part[2 * c + 1]

    pack(0)
    pl.semaphore_wait(barrier, len(peers))
    route = [route_set(0)]

    for copy in load_x:
        copy.wait()
    xts = {}
    for s in (1, 7, 2, 6, 3, 5, 4):
        for h in range(2):
            xts[s, h] = send(
                x.at[((y + s) % RING) * 2 + h], xt.at[s, h], xt_ss.at[s, h], xt_rs.at[s, h], dpy(s)
            )
    for h in range(2):
        xt[0, h] = x[y * 2 + h]

    for r in (1, 2):
        pack(r)
        route.append(route_set(r))

    unpack(0, ((0, 0), (0, 1)))

    def ring_send(buf, ss, rs, k, h, peer, sign):
        src, dst = (k - 1, k) if sign > 0 else ((RING + 1 - k) % RING, RING - k)
        way = 0 if sign > 0 else 1
        return send(buf.at[src, h], buf.at[dst, h], ss.at[way, k - 1, h], rs.at[way, k - 1, h], peer(sign))

    def ring_begin(buf, ss, rs, peer):
        flight = {}
        for h in range(2):
            for sign in (1, -1):
                flight[sign, 1, h] = ring_send(buf, ss, rs, 1, h, peer, sign)
        return flight

    def ring_step(flight, buf, ss, rs, peer, k, h, last):
        for sign in (1, -1):
            flight[sign, k, h].wait_recv()
            if k < last - 1 or h == (0 if sign > 0 else 1):
                flight[sign, k + 1, h] = ring_send(buf, ss, rs, k + 1, h, peer, sign)

    def ring_end(flight, last):
        flight[1, last, 0].wait_recv()
        flight[-1, last, 1].wait_recv()

    flight = ring_begin(routed, tp_ss, tp_rs, tp)

    load_wg.wait()
    load_wu.wait()
    gate = mm(x[0], wg[:H, :], 1, 0)
    upward = mm(x[0], wu[:H, :], 1, 0)
    for j in range(1, 2 * RING):
        gate = gate + mm(x[j], wg[j * H:j * H + H, :], 1, 0)
        upward = upward + mm(x[j], wu[j * H:j * H + H, :], 1, 0)
    sig = 1.0 / (1.0 + jnp.exp(-gate))
    up_factor = gate * sig
    gate_factor = upward * sig * (1.0 + gate * (1.0 - sig))

    load_wd.wait()

    def hidden_term(s, h):
        first = ((t - s + RING) % RING) * FEAT + h * H
        return mm(routed[s, h], wd[:, pl.ds(pl.multiple_of(first, H), H)], 1, 1)

    grad_hidden = hidden_term(0, 0) + hidden_term(0, 1)
    for k in range(1, 3):
        for h in range(2):
            ring_step(flight, routed, tp_ss, tp_rs, tp, k, h, 3)
            grad_hidden = grad_hidden + hidden_term(k, h) + hidden_term(RING - k, h)
    unpack(1, ((4, 0), (4, 1)))
    unpack(2, ((3, 1), (5, 0)))
    for s, h in ((4, 0), (4, 1), (3, 1), (5, 0)):
        grad_hidden = grad_hidden + hidden_term(s, h)
    ring_end(flight, 3)
    grad_hidden = grad_hidden + hidden_term(3, 0) + hidden_term(5, 1)

    grad_gate_pre = (grad_hidden * gate_factor).astype(BF16)
    grad_up_pre = (grad_hidden * up_factor).astype(BF16)
    pa[0, 0] = grad_gate_pre
    pa[0, 1] = grad_up_pre
    dp_flight = ring_begin(pa, dp_ss, dp_rs, dpy)

    def partial_term(j, h):
        first = pl.ds(pl.multiple_of(((t + j) % RING) * FEAT + h * H, H), H)
        part[j, h] = (mm(grad_gate_pre, wg[first, :], 1, 1) + mm(grad_up_pre, wu[first, :], 1, 1)).astype(BF16)

    rs_flight = {}

    def sum_send(sign, k, h):
        way = 0 if sign > 0 else 1
        slot_ = k if sign > 0 else RING - k
        dst = (from_left if sign > 0 else from_right).at[k - 1, h]
        rs_flight[sign, k, h] = send(
            part.at[slot_, h], dst, rs_ss.at[way, k - 1, h], rs_rs.at[way, k - 1, h], tp(sign)
        )

    def sum_step(sign, k, h):
        rs_flight[sign, k + 1, h].wait_recv()
        slot_ = k if sign > 0 else RING - k
        arrived = (from_left if sign > 0 else from_right)[k, h]
        part[slot_, h] = (part[slot_, h].astype(F32) + arrived.astype(F32)).astype(BF16)
        sum_send(sign, k, h)

    partial_term(4, 0)
    sum_send(1, 4, 0)
    partial_term(4, 1)
    sum_send(-1, 4, 1)
    partial_term(3, 1)
    sum_send(1, 3, 1)
    partial_term(5, 0)
    sum_send(-1, 3, 0)
    partial_term(3, 0)
    partial_term(5, 1)

    def dp_step(k, h):
        ring_step(dp_flight, pa, dp_ss, dp_rs, dpy, k, h, 4)

    def weight_term(s):
        if s:
            for h in range(2):
                xts[s, h].wait_recv()
        for half in range(2):
            for which in range(2):
                term = mm(xt[s, half], pa[s, which], 0, 0)
                acc[half, which] = acc[half, which] + term if s else term

    dp_step(1, 0)
    sum_step(1, 3, 0)
    sum_step(-1, 3, 1)
    for j in (2, 6):
        for h in range(2):
            partial_term(j, h)
    dp_step(1, 1)
    sum_step(1, 2, 1)
    sum_step(-1, 2, 0)
    weight_term(0)
    dp_step(2, 0)
    sum_step(1, 2, 0)
    sum_step(-1, 2, 1)
    for j in (1, 7, 0):
        for h in range(2):
            partial_term(j, h)
    dp_step(2, 1)
    sum_step(1, 1, 1)
    sum_step(-1, 1, 0)
    weight_term(1)
    weight_term(7)
    dp_step(3, 0)
    sum_step(1, 1, 0)
    sum_step(-1, 1, 1)
    weight_term(2)
    weight_term(6)
    dp_step(3, 1)
    weight_term(3)
    weight_term(5)
    for h in range(2):
        xts[4, h].wait_recv()
    ring_end(dp_flight, 4)
    w_flight = []
    for which in range(2):
        w_out[which] = (acc[1 - a, which] + mm(xt[4, 1 - a], pa[4, which], 0, 0)).astype(BF16)
        w_flight.append(send(w_out.at[which], w_in.at[which], w_ss.at[which], w_rs.at[which], twin))

    for h in (1, 0):
        rs_flight[1, 1, h].wait_recv()
        rs_flight[-1, 1, h].wait_recv()
    slot_grad = [
        (part[0, h].astype(F32) + from_left[0, h].astype(F32) + from_right[0, h].astype(F32)).astype(BF16)
        for h in range(2)
    ]
    for h in range(2):
        back_out[:, :, h * H:h * H + H] = mm(main_map, slot_grad[h][:TOK, :], 0, 0).astype(BF16).reshape(RING, MAIN, H)
    folded = mm(fold_map[0], slot_grad[0][TOK:, :128], 0, 0)
    for q in range(1, 4):
        folded = folded + mm(fold_map[q], slot_grad[q // 2][TOK:, (q % 2) * 128:(q % 2) * 128 + 128], 0, 0)
    back_out[:, :, FEAT:] = folded.astype(BF16).reshape(RING, MAIN, 128)
    back_in[e] = back_out[e]
    back = [
        send(back_out.at[(e + s) % RING], back_in.at[e], back_ss.at[s], back_rs.at[s], ctx(s)) for s in range(1, RING)
    ]

    own = [acc[a, which] + mm(xt[4, a], pa[4, which], 0, 0) for which in range(2)]

    for copy in back:
        copy.wait_recv()
    main_in = back_in[:, :, :FEAT].reshape(TOK, FEAT)
    fold_in = back_in[:, :, FEAT:].reshape(TOK, 128)
    token_rows = mm(to_main, main_in, 0, 0)
    for q in range(4):
        piece = slice(128 * q, 128 * q + 128)
        gi_out[0, :, piece] = (token_rows[:, piece] + mm(to_fold[q], fold_in, 0, 0)).astype(BF16)

    for which, out in enumerate((gg_out, gu_out)):
        w_flight[which].wait_recv()
        out[0] = (own[which] + w_in[which].astype(F32)) * (1.0 / 16.0)

    for copy in started:
        copy.wait_send()


def flush(gi, gg, gu, gi_out, gg_out, gu_out, sems):
    copies = [
        pltpu.make_async_copy(src, dst, sems.at[n])
        for n, (src, dst) in enumerate(((gi, gi_out), (gg, gg_out), (gu, gu_out)))
    ]
    for copy in copies:
        copy.start()
    for copy in copies:
        copy.wait()


def body(grad_out, expert_input, expert_ids, slots, w_gate, w_up, w_down):
    saved = expert_input.transpose(0, 1, 3, 2, 4).reshape(ROWS, D)
    vmem = pl.BlockSpec(memory_space=pltpu.VMEM)
    hbm = pl.BlockSpec(memory_space=pl.ANY)
    dma = pltpu.SemaphoreType.DMA
    piece = (2, ROWS, H)
    shapes = (((1, TOK, FEAT), BF16), ((1, 256, FB), F32), ((1, 256, FB), F32))
    operands = [
        pltpu.with_memory_space_constraint(operand, pltpu.HBM)
        for operand in (expert_ids, slots, grad_out, saved, w_gate, w_up, w_down)
    ]
    results = pl.pallas_call(
        kernel,
        out_shape=tuple(pltpu.VMEM(shape, dtype) for shape, dtype in shapes),
        in_specs=[hbm] * 7,
        out_specs=(vmem, vmem, vmem),
        scratch_shapes=[
            pltpu.VMEM((1, TOK), jnp.int32),
            pltpu.VMEM((1, TOK), jnp.int32),
            pltpu.VMEM((3, 2, TOK, H), BF16),
            pltpu.VMEM((2 * RING, ROWS, H), BF16),
            pltpu.VMEM((D, FB), BF16),
            pltpu.VMEM((D, FB), BF16),
            pltpu.VMEM((FB, D), BF16),
            pltpu.VMEM((3, RING, MAIN, PACK), BF16),
            pltpu.VMEM((3, RING, MAIN, PACK), BF16),
            pltpu.VMEM((RING,) + piece, BF16),
            pltpu.VMEM((RING,) + piece, BF16),
            pltpu.VMEM((RING,) + piece, BF16),
            pltpu.VMEM((RING,) + piece, BF16),
            pltpu.VMEM((4,) + piece, BF16),
            pltpu.VMEM((4,) + piece, BF16),
            pltpu.VMEM((RING, MAIN, PACK), BF16),
            pltpu.VMEM((RING, MAIN, PACK), BF16),
            pltpu.VMEM((2, 256, FB), BF16),
            pltpu.VMEM((2, 256, FB), BF16),
            pltpu.VMEM((2, 2, 256, FB), F32),
            dma((6,)),
            dma((3, 2)),
            dma((2 * RING,)),
            dma((3, RING)),
            dma((3, RING)),
            dma((RING, 2)),
            dma((RING, 2)),
            dma((2, 4, 2)),
            dma((2, 4, 2)),
            dma((2, 4, 2)),
            dma((2, 4, 2)),
            dma((2, 4, 2)),
            dma((2, 4, 2)),
            dma((RING,)),
            dma((RING,)),
            dma((2,)),
            dma((2,)),
        ],
        compiler_params=pltpu.CompilerParams(
            collective_id=0, has_side_effects=True, vmem_limit_bytes=40 * 1024 * 1024
        ),
        name="expert_backward",
    )(*operands)
    return pl.pallas_call(
        flush,
        out_shape=tuple(jax.ShapeDtypeStruct(shape, dtype) for shape, dtype in shapes),
        in_specs=[hbm] * 3,
        out_specs=(hbm, hbm, hbm),
        scratch_shapes=[dma((3,))],
        name="write_results",
    )(*results)


def solution(mesh):
    return jax.shard_map(
        body,
        mesh=mesh,
        in_specs=(
            P("dp", "ctx", None),
            P("ctx", "dp", None, None, None),
            P("dp", "ctx"),
            P("dp", "ctx"),
            P("ctx", None, "tp"),
            P("ctx", None, "tp"),
            P("ctx", "tp", None),
        ),
        out_specs=(P("dp", "ctx", "tp"), P("ctx", "dp", "tp"), P("ctx", "dp", "tp")),
        check_vma=False,
    )
```

```python
import jax
import jax.numpy as jnp
from jax import lax
from jax.experimental import pallas as pl
from jax.experimental.pallas import tpu as pltpu
from jax.sharding import PartitionSpec as P

MESH = pl.DeviceIdType.MESH
BF16 = jnp.bfloat16
F32 = jnp.float32

RING = 8
CAP = 19
ROWS = RING * CAP
MAIN = 16
TOK = 128
D = 4096
FEAT = D // RING
H = FEAT // 2
FB = 256
PACK = FEAT + 128
SETS = 2
SHARED = (4,)


def mm(a, b, ca, cb):
    return lax.dot_general(a, b, (((ca,), (cb,)), ((), ())), preferred_element_type=F32)


def iota(shape, dim):
    return lax.broadcasted_iota(jnp.int32, shape, dim)


def onehot(mask):
    return jnp.where(mask, 1.0, 0.0).astype(BF16)


def kernel(
    ids_hbm, slots_hbm, tok_hbm, x_hbm, wg_hbm, wu_hbm, wd_hbm,
    gi_out, gg_out, gu_out,
    ids, slots, tok, x, wg, wu, wd, route_out, route_in, routed, xt, pa, part, from_left, from_right, back_out, back_in, w_out, w_in, acc,
    load_sem, tok_sem, xload_sem,
    route_ss, route_rs, xt_ss, xt_rs, share_ss, share_rs, tp_ss, tp_rs, dp_ss, dp_rs, rs_ss, rs_rs, back_ss, back_rs, w_ss, w_rs,
):
    e, t, d = lax.axis_index("ctx"), lax.axis_index("tp"), lax.axis_index("dp")
    y, a = d // 2, d % 2

    def ctx(s):
        return {"ctx": (e + s) % RING}

    def tp(s):
        return {"tp": (t + s + RING) % RING}

    def dpy(s):
        return {"dp": ((y + s + RING) % RING) * 2 + a}

    over = {"tp": (t + 2 - 4 * (t % 4 // 2) + RING) % RING}
    twin = {"dp": y * 2 + 1 - a}
    started = []

    def send(src, dst, ss, rs, dev):
        copy = pltpu.make_async_remote_copy(
            src_ref=src, dst_ref=dst, send_sem=ss, recv_sem=rs, device_id=dev, device_id_type=MESH
        )
        copy.start()
        started.append(copy)
        return copy

    load_ids = pltpu.make_async_copy(ids_hbm, ids, load_sem.at[4])
    load_slots = pltpu.make_async_copy(slots_hbm, slots, load_sem.at[5])
    load_ids.start()
    load_slots.start()
    load_tok = []
    for r, c in ((0, 0), (0, 1), (1, 0), (1, 1))[:2 * SETS]:
        first = (t + 4 * r) % RING * 2 + c
        load_tok.append(
            pltpu.make_async_copy(
                tok_hbm.at[0, :, pl.ds(pl.multiple_of(first * H, H), H)], tok.at[r, c], tok_sem.at[r, c]
            )
        )
        load_tok[-1].start()
    load_x = [
        pltpu.make_async_copy(x_hbm.at[:, pl.ds(j * H, H)], x.at[j], xload_sem.at[j]) for j in range(2 * RING)
    ]
    for copy in load_x:
        copy.start()
    load_wg = pltpu.make_async_copy(wg_hbm.at[0], wg, load_sem.at[1])
    load_wu = pltpu.make_async_copy(wu_hbm.at[0], wu, load_sem.at[2])
    load_wd = pltpu.make_async_copy(wd_hbm.at[0], wd, load_sem.at[3])
    load_wg.start()
    load_wu.start()
    load_wd.start()

    barrier = pltpu.get_barrier_semaphore()
    peers = [ctx(s) for s in range(1, RING)] + [tp(1), tp(-1)] + [dpy(s) for s in range(1, RING)] + [over, twin]
    for peer in peers:
        pl.semaphore_signal(barrier, inc=1, device_id=peer, device_id_type=MESH)

    load_ids.wait()
    load_slots.wait()
    expert, slot = ids[...], slots[...]
    main_row = jnp.where(slot < MAIN, expert * MAIN + slot, -1)
    fold_row = jnp.where(slot < MAIN, -8, expert * MAIN + 4 * (slot - MAIN))
    rows = iota((TOK, TOK), 0)
    to_main = onehot(rows == main_row)
    to_fold = [onehot(rows == fold_row + q) for q in range(4)]
    cols = iota((TOK, TOK), 1)
    main_map = onehot(cols == (rows % RING) * MAIN + rows // RING)
    erow = iota((3 * RING, TOK), 0)
    ecol = iota((3 * RING, TOK), 1)
    fold_map = [onehot(ecol == (erow % RING) * MAIN + 4 * (erow // RING) + q) for q in range(4)]

    def pack(r):
        load_tok[2 * r].wait()
        load_tok[2 * r + 1].wait()
        halves = [tok[r, c] for c in range(2)]
        for c in range(2):
            route_out[r, :, :, c * H:c * H + H] = mm(to_main, halves[c], 1, 0).astype(BF16).reshape(RING, MAIN, H)
        folded = mm(to_fold[0], halves[0][:, :128], 1, 0)
        for q in range(1, 4):
            folded = folded + mm(to_fold[q], halves[q // 2][:, (q % 2) * 128:(q % 2) * 128 + 128], 1, 0)
        route_out[r, :, :, FEAT:] = folded.astype(BF16).reshape(RING, MAIN, 128)
        route_in[r, e] = route_out[r, e]

    def route_set(r):
        return [
            send(
                route_out.at[r, (e + s) % RING], route_in.at[r, e], route_ss.at[r, s], route_rs.at[r, s], ctx(s)
            )
            for s in range(1, RING)
        ]

    def unpack(r, places):
        for copy in route[r]:
            copy.wait_recv()
        main_in = route_in[r, :, :, :FEAT].reshape(TOK, FEAT)
        fold_in = route_in[r, :, :, FEAT:].reshape(TOK, 128)
        main_part = mm(main_map, main_in, 1, 0).astype(BF16)
        fold_part = [mm(m, fold_in, 1, 0).astype(BF16) for m in fold_map]
        for c, (s, h) in enumerate(places):
            routed[s, h, :TOK, :] = main_part[:, c * H:c * H + H]
            routed[s, h, TOK:, :128] = fold_part[2 * c]
            routed[s, h, TOK:, 128:] = fold_part[2 * c + 1]

    pack(0)
    pl.semaphore_wait(barrier, len(peers))
    route = [route_set(0)]

    for copy in load_x:
        copy.wait()
    quarter = t % 4
    lanes = pl.ds(pl.multiple_of(quarter % 2 * 128, 128), 128)
    quarters, xts, shares = {}, {}, {}
    for s in SHARED:
        quarters[s] = send(
            x.at[((y + s) % RING) * 2 + quarter // 2, :, lanes], xt.at[s, quarter // 2, :, lanes],
            xt_ss.at[s, 0], xt_rs.at[s, 0], dpy(s),
        )
    for s in (1, 7, 2, 6, 3, 5, 4):
        for h in range(2):
            if s not in SHARED:
                xts[s, h] = send(
                    x.at[((y + s) % RING) * 2 + h], xt.at[s, h], xt_ss.at[s, h], xt_rs.at[s, h], dpy(s)
                )
    for h in range(2):
        xt[0, h] = x[y * 2 + h]

    def share():
        for s in SHARED:
            quarters[s].wait_recv()
            piece = xt.at[s, quarter // 2, :, lanes]
            shares[s] = [
                send(piece, piece, share_ss.at[s, n], share_rs.at[s, n], peer)
                for n, peer in enumerate((tp(1), tp(-1), over))
            ]

    def saved_arrived(s):
        if s in SHARED:
            for copy in shares[s]:
                copy.wait_recv()
        elif s:
            for h in range(2):
                xts[s, h].wait_recv()

    for r in range(1, SETS):
        pack(r)
        route.append(route_set(r))

    unpack(0, ((0, 0), (0, 1)))

    def ring_send(buf, ss, rs, k, h, peer, sign):
        src, dst = (k - 1, k) if sign > 0 else ((RING + 1 - k) % RING, RING - k)
        way = 0 if sign > 0 else 1
        return send(buf.at[src, h], buf.at[dst, h], ss.at[way, k - 1, h], rs.at[way, k - 1, h], peer(sign))

    def ring_begin(buf, ss, rs, peer):
        flight = {}
        for h in range(2):
            for sign in (1, -1):
                flight[sign, 1, h] = ring_send(buf, ss, rs, 1, h, peer, sign)
        return flight

    def ring_step(flight, buf, ss, rs, peer, k, h, part_):
        for sign in (1, -1):
            flight[sign, k, h].wait_recv()
            if k < 3 or (part_ and h == (0 if sign > 0 else 1)):
                flight[sign, k + 1, h] = ring_send(buf, ss, rs, k + 1, h, peer, sign)

    def ring_end(flight):
        flight[1, 4, 0].wait_recv()
        flight[-1, 4, 1].wait_recv()

    flight = ring_begin(routed, tp_ss, tp_rs, tp)

    load_wg.wait()
    load_wu.wait()
    gate = mm(x[0], wg[:H, :], 1, 0)
    upward = mm(x[0], wu[:H, :], 1, 0)
    for j in range(1, 2 * RING):
        gate = gate + mm(x[j], wg[j * H:j * H + H, :], 1, 0)
        upward = upward + mm(x[j], wu[j * H:j * H + H, :], 1, 0)
    sig = 1.0 / (1.0 + jnp.exp(-gate))
    up_factor = gate * sig
    gate_factor = upward * sig * (1.0 + gate * (1.0 - sig))

    load_wd.wait()

    def hidden_term(s, h):
        first = ((t - s + RING) % RING) * FEAT + h * H
        return mm(routed[s, h], wd[:, pl.ds(pl.multiple_of(first, H), H)], 1, 1)

    grad_hidden = hidden_term(0, 0) + hidden_term(0, 1)
    for k in range(1, 4):
        for h in range(2):
            ring_step(flight, routed, tp_ss, tp_rs, tp, k, h, SETS == 1)
            grad_hidden = grad_hidden + hidden_term(k, h) + hidden_term(RING - k, h)
        if k == 2 and SETS > 1:
            unpack(1, ((4, 0), (4, 1)))
            grad_hidden = grad_hidden + hidden_term(4, 0) + hidden_term(4, 1)
    if SETS == 1:
        ring_end(flight)
        grad_hidden = grad_hidden + hidden_term(4, 0) + hidden_term(4, 1)

    grad_gate_pre = (grad_hidden * gate_factor).astype(BF16)
    grad_up_pre = (grad_hidden * up_factor).astype(BF16)
    pa[0, 0] = grad_gate_pre
    pa[0, 1] = grad_up_pre
    dp_flight = ring_begin(pa, dp_ss, dp_rs, dpy)
    share()

    def partial_term(j, h):
        first = pl.ds(pl.multiple_of(((t + j) % RING) * FEAT + h * H, H), H)
        part[j, h] = (mm(grad_gate_pre, wg[first, :], 1, 1) + mm(grad_up_pre, wu[first, :], 1, 1)).astype(BF16)

    rs_flight = {}

    def sum_send(sign, k, h):
        way = 0 if sign > 0 else 1
        slot_ = k if sign > 0 else RING - k
        dst = (from_left if sign > 0 else from_right).at[k - 1, h]
        rs_flight[sign, k, h] = send(
            part.at[slot_, h], dst, rs_ss.at[way, k - 1, h], rs_rs.at[way, k - 1, h], tp(sign)
        )

    def sum_step(sign, k, h):
        rs_flight[sign, k + 1, h].wait_recv()
        slot_ = k if sign > 0 else RING - k
        arrived = (from_left if sign > 0 else from_right)[k, h]
        part[slot_, h] = (part[slot_, h].astype(F32) + arrived.astype(F32)).astype(BF16)
        sum_send(sign, k, h)

    partial_term(4, 0)
    sum_send(1, 4, 0)
    partial_term(4, 1)
    sum_send(-1, 4, 1)
    partial_term(3, 1)
    sum_send(1, 3, 1)
    partial_term(5, 0)
    sum_send(-1, 3, 0)
    partial_term(3, 0)
    partial_term(5, 1)

    def dp_step(k, h):
        ring_step(dp_flight, pa, dp_ss, dp_rs, dpy, k, h, True)

    def weight_term(s):
        saved_arrived(s)
        for half in range(2):
            for which in range(2):
                term = mm(xt[s, half], pa[s, which], 0, 0)
                acc[half, which] = acc[half, which] + term if s else term

    dp_step(1, 0)
    sum_step(1, 3, 0)
    sum_step(-1, 3, 1)
    for j in (2, 6):
        for h in range(2):
            partial_term(j, h)
    dp_step(1, 1)
    sum_step(1, 2, 1)
    sum_step(-1, 2, 0)
    weight_term(0)
    dp_step(2, 0)
    sum_step(1, 2, 0)
    sum_step(-1, 2, 1)
    for j in (1, 7, 0):
        for h in range(2):
            partial_term(j, h)
    dp_step(2, 1)
    sum_step(1, 1, 1)
    sum_step(-1, 1, 0)
    weight_term(1)
    weight_term(7)
    dp_step(3, 0)
    sum_step(1, 1, 0)
    sum_step(-1, 1, 1)
    weight_term(2)
    weight_term(6)
    dp_step(3, 1)
    weight_term(3)
    weight_term(5)
    saved_arrived(4)
    ring_end(dp_flight)
    w_flight = []
    for which in range(2):
        w_out[which] = (acc[1 - a, which] + mm(xt[4, 1 - a], pa[4, which], 0, 0)).astype(BF16)
        w_flight.append(send(w_out.at[which], w_in.at[which], w_ss.at[which], w_rs.at[which], twin))

    for h in (1, 0):
        rs_flight[1, 1, h].wait_recv()
        rs_flight[-1, 1, h].wait_recv()
    slot_grad = [
        (part[0, h].astype(F32) + from_left[0, h].astype(F32) + from_right[0, h].astype(F32)).astype(BF16)
        for h in range(2)
    ]
    for h in range(2):
        back_out[:, :, h * H:h * H + H] = mm(main_map, slot_grad[h][:TOK, :], 0, 0).astype(BF16).reshape(RING, MAIN, H)
    folded = mm(fold_map[0], slot_grad[0][TOK:, :128], 0, 0)
    for q in range(1, 4):
        folded = folded + mm(fold_map[q], slot_grad[q // 2][TOK:, (q % 2) * 128:(q % 2) * 128 + 128], 0, 0)
    back_out[:, :, FEAT:] = folded.astype(BF16).reshape(RING, MAIN, 128)
    back_in[e] = back_out[e]
    back = [
        send(back_out.at[(e + s) % RING], back_in.at[e], back_ss.at[s], back_rs.at[s], ctx(s)) for s in range(1, RING)
    ]

    own = [acc[a, which] + mm(xt[4, a], pa[4, which], 0, 0) for which in range(2)]

    for copy in back:
        copy.wait_recv()
    main_in = back_in[:, :, :FEAT].reshape(TOK, FEAT)
    fold_in = back_in[:, :, FEAT:].reshape(TOK, 128)
    token_rows = mm(to_main, main_in, 0, 0)
    for q in range(4):
        piece = slice(128 * q, 128 * q + 128)
        gi_out[0, :, piece] = (token_rows[:, piece] + mm(to_fold[q], fold_in, 0, 0)).astype(BF16)

    for which, out in enumerate((gg_out, gu_out)):
        w_flight[which].wait_recv()
        out[0] = (own[which] + w_in[which].astype(F32)) * (1.0 / 16.0)

    for copy in started:
        copy.wait_send()


def body(grad_out, expert_input, expert_ids, slots, w_gate, w_up, w_down):
    saved = expert_input.transpose(0, 1, 3, 2, 4).reshape(ROWS, D)
    vmem = pl.BlockSpec(memory_space=pltpu.VMEM)
    hbm = pl.BlockSpec(memory_space=pl.ANY)
    dma = pltpu.SemaphoreType.DMA
    piece = (2, ROWS, H)
    shapes = (((1, TOK, FEAT), BF16), ((1, 256, FB), F32), ((1, 256, FB), F32))
    operands = [
        pltpu.with_memory_space_constraint(operand, pltpu.HBM)
        for operand in (expert_ids, slots, grad_out, saved, w_gate, w_up, w_down)
    ]
    return pl.pallas_call(
        kernel,
        out_shape=tuple(pltpu.VMEM(shape, dtype) for shape, dtype in shapes),
        in_specs=[hbm] * 7,
        out_specs=(vmem, vmem, vmem),
        scratch_shapes=[
            pltpu.VMEM((1, TOK), jnp.int32),
            pltpu.VMEM((1, TOK), jnp.int32),
            pltpu.VMEM((SETS, 2, TOK, H), BF16),
            pltpu.VMEM((2 * RING, ROWS, H), BF16),
            pltpu.VMEM((D, FB), BF16),
            pltpu.VMEM((D, FB), BF16),
            pltpu.VMEM((FB, D), BF16),
            pltpu.VMEM((SETS, RING, MAIN, PACK), BF16),
            pltpu.VMEM((SETS, RING, MAIN, PACK), BF16),
            pltpu.VMEM((RING,) + piece, BF16),
            pltpu.VMEM((RING,) + piece, BF16),
            pltpu.VMEM((RING,) + piece, BF16),
            pltpu.VMEM((RING,) + piece, BF16),
            pltpu.VMEM((4,) + piece, BF16),
            pltpu.VMEM((4,) + piece, BF16),
            pltpu.VMEM((RING, MAIN, PACK), BF16),
            pltpu.VMEM((RING, MAIN, PACK), BF16),
            pltpu.VMEM((2, 256, FB), BF16),
            pltpu.VMEM((2, 256, FB), BF16),
            pltpu.VMEM((2, 2, 256, FB), F32),
            dma((6,)),
            dma((SETS, 2)),
            dma((2 * RING,)),
            dma((SETS, RING)),
            dma((SETS, RING)),
            dma((RING, 2)),
            dma((RING, 2)),
            dma((RING, 3)),
            dma((RING, 3)),
            dma((2, 4, 2)),
            dma((2, 4, 2)),
            dma((2, 4, 2)),
            dma((2, 4, 2)),
            dma((2, 4, 2)),
            dma((2, 4, 2)),
            dma((RING,)),
            dma((RING,)),
            dma((2,)),
            dma((2,)),
        ],
        compiler_params=pltpu.CompilerParams(
            collective_id=0, has_side_effects=True, vmem_limit_bytes=40 * 1024 * 1024
        ),
        name="expert_backward",
    )(*operands)


def solution(mesh):
    return jax.shard_map(
        body,
        mesh=mesh,
        in_specs=(
            P("dp", "ctx", None),
            P("ctx", "dp", None, None, None),
            P("dp", "ctx"),
            P("dp", "ctx"),
            P("ctx", None, "tp"),
            P("ctx", None, "tp"),
            P("ctx", "tp", None),
        ),
        out_specs=(P("dp", "ctx", "tp"), P("ctx", "dp", "tp"), P("ctx", "dp", "tp")),
        check_vma=False,
    )
```

```python
import jax
import jax.numpy as jnp
from jax import lax
from jax.experimental import pallas as pl
from jax.experimental.pallas import tpu as pltpu
from jax.sharding import PartitionSpec as P

MESH = pl.DeviceIdType.MESH
BF16 = jnp.bfloat16
F32 = jnp.float32

RING = 8
CAP = 19
ROWS = RING * CAP
MAIN = 16
TOK = 128
D = 4096
FEAT = D // RING
H = FEAT // 2
FB = 256
PACK = FEAT + 128
SETS = 2
SHARED = (4,)


def mm(a, b, ca, cb):
    return lax.dot_general(a, b, (((ca,), (cb,)), ((), ())), preferred_element_type=F32)


def iota(shape, dim):
    return lax.broadcasted_iota(jnp.int32, shape, dim)


def onehot(mask):
    return jnp.where(mask, 1.0, 0.0).astype(BF16)


def kernel(
    ids_hbm, slots_hbm, tok_hbm, x_hbm, wg_hbm, wu_hbm, wd_hbm,
    gi_out, gg_out, gu_out,
    ids, slots, tok, x, wg, wu, wd, route_out, route_in, routed, xt, pa, part, from_left, from_right, back_out, back_in, w_out, w_in, acc,
    load_sem, tok_sem, xload_sem,
    route_ss, route_rs, xt_ss, xt_rs, share_ss, share_rs, tp_ss, tp_rs, dp_ss, dp_rs, rs_ss, rs_rs, back_ss, back_rs, w_ss, w_rs,
):
    e, t, d = lax.axis_index("ctx"), lax.axis_index("tp"), lax.axis_index("dp")
    y, a = d // 2, d % 2

    def ctx(s):
        return {"ctx": (e + s) % RING}

    def tp(s):
        return {"tp": (t + s + RING) % RING}

    def dpy(s):
        return {"dp": ((y + s + RING) % RING) * 2 + a}

    over = {"tp": (t + 2 - 4 * (t % 4 // 2) + RING) % RING}
    twin = {"dp": y * 2 + 1 - a}
    started = []

    def send(src, dst, ss, rs, dev):
        copy = pltpu.make_async_remote_copy(
            src_ref=src, dst_ref=dst, send_sem=ss, recv_sem=rs, device_id=dev, device_id_type=MESH
        )
        copy.start()
        started.append(copy)
        return copy

    load_ids = pltpu.make_async_copy(ids_hbm, ids, load_sem.at[4])
    load_slots = pltpu.make_async_copy(slots_hbm, slots, load_sem.at[5])
    load_ids.start()
    load_slots.start()
    load_tok = []
    for r, c in ((0, 0), (0, 1), (1, 0), (1, 1))[:2 * SETS]:
        first = (t + 4 * r) % RING * 2 + c
        load_tok.append(
            pltpu.make_async_copy(
                tok_hbm.at[0, :, pl.ds(pl.multiple_of(first * H, H), H)], tok.at[r, c], tok_sem.at[r, c]
            )
        )
        load_tok[-1].start()
    barrier = pltpu.get_barrier_semaphore()
    peers = [ctx(s) for s in range(1, RING)] + [tp(1), tp(-1)] + [dpy(s) for s in range(1, RING)] + [over, twin]
    for peer in peers:
        pl.semaphore_signal(barrier, inc=1, device_id=peer, device_id_type=MESH)

    load_x = [
        pltpu.make_async_copy(x_hbm.at[:, pl.ds(j * H, H)], x.at[j], xload_sem.at[j]) for j in range(2 * RING)
    ]
    for copy in load_x:
        copy.start()
    load_wg = pltpu.make_async_copy(wg_hbm.at[0], wg, load_sem.at[1])
    load_wu = pltpu.make_async_copy(wu_hbm.at[0], wu, load_sem.at[2])
    load_wd = pltpu.make_async_copy(wd_hbm.at[0], wd, load_sem.at[3])
    load_wg.start()
    load_wu.start()
    load_wd.start()

    rows = iota((TOK, TOK), 0)
    cols = iota((TOK, TOK), 1)
    main_map = onehot(cols == (rows % RING) * MAIN + rows // RING)
    erow = iota((3 * RING, TOK), 0)
    ecol = iota((3 * RING, TOK), 1)
    fold_map = [onehot(ecol == (erow % RING) * MAIN + 4 * (erow // RING) + q) for q in range(4)]

    load_ids.wait()
    load_slots.wait()
    expert, slot = ids[...], slots[...]
    main_row = jnp.where(slot < MAIN, expert * MAIN + slot, -1)
    fold_row = jnp.where(slot < MAIN, -8, expert * MAIN + 4 * (slot - MAIN))
    to_main = onehot(rows == main_row)
    to_fold = [onehot(rows == fold_row + q) for q in range(4)]
    def pack(r):
        load_tok[2 * r].wait()
        load_tok[2 * r + 1].wait()
        halves = [tok[r, c] for c in range(2)]
        for c in range(2):
            route_out[r, :, :, c * H:c * H + H] = mm(to_main, halves[c], 1, 0).astype(BF16).reshape(RING, MAIN, H)
        folded = mm(to_fold[0], halves[0][:, :128], 1, 0)
        for q in range(1, 4):
            folded = folded + mm(to_fold[q], halves[q // 2][:, (q % 2) * 128:(q % 2) * 128 + 128], 1, 0)
        route_out[r, :, :, FEAT:] = folded.astype(BF16).reshape(RING, MAIN, 128)
        route_in[r, e] = route_out[r, e]

    def route_set(r):
        return [
            send(
                route_out.at[r, (e + s) % RING], route_in.at[r, e], route_ss.at[r, s], route_rs.at[r, s], ctx(s)
            )
            for s in range(1, RING)
        ]

    def unpack(r, places):
        for copy in route[r]:
            copy.wait_recv()
        main_in = route_in[r, :, :, :FEAT].reshape(TOK, FEAT)
        fold_in = route_in[r, :, :, FEAT:].reshape(TOK, 128)
        main_part = mm(main_map, main_in, 1, 0).astype(BF16)
        fold_part = [mm(m, fold_in, 1, 0).astype(BF16) for m in fold_map]
        for c, (s, h) in enumerate(places):
            routed[s, h, :TOK, :] = main_part[:, c * H:c * H + H]
            routed[s, h, TOK:, :128] = fold_part[2 * c]
            routed[s, h, TOK:, 128:] = fold_part[2 * c + 1]

    for r in range(SETS):
        pack(r)
    pl.semaphore_wait(barrier, len(peers))
    route = [route_set(0)]

    for copy in load_x:
        copy.wait()
    quarter = t % 4
    lanes = pl.ds(pl.multiple_of(quarter % 2 * 128, 128), 128)
    quarters, xts, shares = {}, {}, {}
    for s in SHARED:
        quarters[s] = send(
            x.at[((y + s) % RING) * 2 + quarter // 2, :, lanes], xt.at[s, quarter // 2, :, lanes],
            xt_ss.at[s, 0], xt_rs.at[s, 0], dpy(s),
        )
    for s in (1, 7, 2, 6, 3, 5, 4):
        for h in range(2):
            if s not in SHARED:
                xts[s, h] = send(
                    x.at[((y + s) % RING) * 2 + h], xt.at[s, h], xt_ss.at[s, h], xt_rs.at[s, h], dpy(s)
                )
    for h in range(2):
        xt[0, h] = x[y * 2 + h]

    def share():
        for s in SHARED:
            quarters[s].wait_recv()
            piece = xt.at[s, quarter // 2, :, lanes]
            shares[s] = [
                send(piece, piece, share_ss.at[s, n], share_rs.at[s, n], peer)
                for n, peer in enumerate((tp(1), tp(-1), over))
            ]

    def saved_arrived(s):
        if s in SHARED:
            for copy in shares[s]:
                copy.wait_recv()
        elif s:
            for h in range(2):
                xts[s, h].wait_recv()

    unpack(0, ((0, 0), (0, 1)))

    def ring_send(buf, ss, rs, k, h, peer, sign):
        src, dst = (k - 1, k) if sign > 0 else ((RING + 1 - k) % RING, RING - k)
        way = 0 if sign > 0 else 1
        return send(buf.at[src, h], buf.at[dst, h], ss.at[way, k - 1, h], rs.at[way, k - 1, h], peer(sign))

    def ring_begin(buf, ss, rs, peer):
        flight = {}
        for h in range(2):
            for sign in (1, -1):
                flight[sign, 1, h] = ring_send(buf, ss, rs, 1, h, peer, sign)
        return flight

    def ring_step(flight, buf, ss, rs, peer, k, h, part_):
        for sign in (1, -1):
            flight[sign, k, h].wait_recv()
            if k < 3 or (part_ and h == (0 if sign > 0 else 1)):
                flight[sign, k + 1, h] = ring_send(buf, ss, rs, k + 1, h, peer, sign)

    def ring_end(flight):
        flight[1, 4, 0].wait_recv()
        flight[-1, 4, 1].wait_recv()

    flight = ring_begin(routed, tp_ss, tp_rs, tp)
    for r in range(1, SETS):
        route.append(route_set(r))

    load_wg.wait()
    load_wu.wait()
    gate = mm(x[0], wg[:H, :], 1, 0)
    upward = mm(x[0], wu[:H, :], 1, 0)
    for j in range(1, 2 * RING):
        gate = gate + mm(x[j], wg[j * H:j * H + H, :], 1, 0)
        upward = upward + mm(x[j], wu[j * H:j * H + H, :], 1, 0)
    sig = 1.0 / (1.0 + jnp.exp(-gate))
    up_factor = gate * sig
    gate_factor = upward * sig * (1.0 + gate * (1.0 - sig))

    load_wd.wait()

    def hidden_term(s, h):
        first = ((t - s + RING) % RING) * FEAT + h * H
        return mm(routed[s, h], wd[:, pl.ds(pl.multiple_of(first, H), H)], 1, 1)

    grad_hidden = hidden_term(0, 0) + hidden_term(0, 1)
    for k in range(1, 4):
        for h in range(2):
            ring_step(flight, routed, tp_ss, tp_rs, tp, k, h, SETS == 1)
            grad_hidden = grad_hidden + hidden_term(k, h) + hidden_term(RING - k, h)
        if k == 2 and SETS > 1:
            unpack(1, ((4, 0), (4, 1)))
            grad_hidden = grad_hidden + hidden_term(4, 0) + hidden_term(4, 1)
    if SETS == 1:
        ring_end(flight)
        grad_hidden = grad_hidden + hidden_term(4, 0) + hidden_term(4, 1)

    grad_gate_pre = (grad_hidden * gate_factor).astype(BF16)
    grad_up_pre = (grad_hidden * up_factor).astype(BF16)
    pa[0, 0] = grad_gate_pre
    pa[0, 1] = grad_up_pre
    dp_flight = ring_begin(pa, dp_ss, dp_rs, dpy)

    def partial_term(j, h):
        first = pl.ds(pl.multiple_of(((t + j) % RING) * FEAT + h * H, H), H)
        part[j, h] = (mm(grad_gate_pre, wg[first, :], 1, 1) + mm(grad_up_pre, wu[first, :], 1, 1)).astype(BF16)

    rs_flight = {}

    def sum_send(sign, k, h):
        way = 0 if sign > 0 else 1
        slot_ = k if sign > 0 else RING - k
        dst = (from_left if sign > 0 else from_right).at[k - 1, h]
        rs_flight[sign, k, h] = send(
            part.at[slot_, h], dst, rs_ss.at[way, k - 1, h], rs_rs.at[way, k - 1, h], tp(sign)
        )

    def sum_step(sign, k, h):
        rs_flight[sign, k + 1, h].wait_recv()
        slot_ = k if sign > 0 else RING - k
        arrived = (from_left if sign > 0 else from_right)[k, h]
        part[slot_, h] = (part[slot_, h].astype(F32) + arrived.astype(F32)).astype(BF16)
        sum_send(sign, k, h)

    partial_term(4, 0)
    sum_send(1, 4, 0)
    partial_term(4, 1)
    sum_send(-1, 4, 1)
    partial_term(3, 1)
    sum_send(1, 3, 1)
    partial_term(5, 0)
    sum_send(-1, 3, 0)
    share()
    partial_term(3, 0)
    partial_term(5, 1)

    def dp_step(k, h):
        ring_step(dp_flight, pa, dp_ss, dp_rs, dpy, k, h, True)

    def weight_term(s):
        saved_arrived(s)
        for half in range(2):
            for which in range(2):
                term = mm(xt[s, half], pa[s, which], 0, 0)
                acc[half, which] = acc[half, which] + term if s else term

    dp_step(1, 0)
    sum_step(1, 3, 0)
    sum_step(-1, 3, 1)
    for j in (2, 6):
        for h in range(2):
            partial_term(j, h)
    dp_step(1, 1)
    sum_step(1, 2, 1)
    sum_step(-1, 2, 0)
    weight_term(0)
    dp_step(2, 0)
    sum_step(1, 2, 0)
    sum_step(-1, 2, 1)
    for j in (1, 7, 0):
        for h in range(2):
            partial_term(j, h)
    dp_step(2, 1)
    sum_step(1, 1, 1)
    sum_step(-1, 1, 0)
    weight_term(1)
    weight_term(7)
    dp_step(3, 0)
    sum_step(1, 1, 0)
    sum_step(-1, 1, 1)
    weight_term(2)
    weight_term(6)
    dp_step(3, 1)
    weight_term(3)
    weight_term(5)
    def prepared(src, dst, ss, rs, dev):
        return pltpu.make_async_remote_copy(
            src_ref=src, dst_ref=dst, send_sem=ss, recv_sem=rs, device_id=dev, device_id_type=MESH
        )

    sent = len(started)
    w_flight = [
        prepared(w_out.at[which], w_in.at[which], w_ss.at[which], w_rs.at[which], twin) for which in range(2)
    ]
    back = [
        prepared(back_out.at[(e + s) % RING], back_in.at[e], back_ss.at[s], back_rs.at[s], ctx(s))
        for s in range(1, RING)
    ]
    started.extend(w_flight + back)

    def send_weights():
        saved_arrived(4)
        ring_end(dp_flight)
        for which in range(2):
            w_out[which] = (acc[1 - a, which] + mm(xt[4, 1 - a], pa[4, which], 0, 0)).astype(BF16)
            w_flight[which].start()

    def send_back():
        for h in (1, 0):
            rs_flight[1, 1, h].wait_recv()
            rs_flight[-1, 1, h].wait_recv()
        slot_grad = [
            (part[0, h].astype(F32) + from_left[0, h].astype(F32) + from_right[0, h].astype(F32)).astype(BF16)
            for h in range(2)
        ]
        for h in range(2):
            main_rows = mm(main_map, slot_grad[h][:TOK, :], 0, 0).astype(BF16)
            back_out[:, :, h * H:h * H + H] = main_rows.reshape(RING, MAIN, H)
        folded = mm(fold_map[0], slot_grad[0][TOK:, :128], 0, 0)
        for q in range(1, 4):
            folded = folded + mm(fold_map[q], slot_grad[q // 2][TOK:, (q % 2) * 128:(q % 2) * 128 + 128], 0, 0)
        back_out[:, :, FEAT:] = folded.astype(BF16).reshape(RING, MAIN, 128)
        for copy in back:
            copy.start()
        back_in[e] = back_out[e]

    @pl.when(a == 1)
    def weights_first():
        send_weights()
        send_back()

    @pl.when(a == 0)
    def back_first():
        send_back()
        send_weights()

    for copy in started[:sent]:
        copy.wait_send()
    own = [acc[a, which] + mm(xt[4, a], pa[4, which], 0, 0) for which in range(2)]

    for copy in back:
        copy.wait_recv()
    main_in = back_in[:, :, :FEAT].reshape(TOK, FEAT)
    fold_in = back_in[:, :, FEAT:].reshape(TOK, 128)
    token_rows = mm(to_main, main_in, 0, 0)
    for q in range(4):
        piece = slice(128 * q, 128 * q + 128)
        gi_out[0, :, piece] = (token_rows[:, piece] + mm(to_fold[q], fold_in, 0, 0)).astype(BF16)

    for which, out in enumerate((gg_out, gu_out)):
        w_flight[which].wait_recv()
        out[0] = (own[which] + w_in[which].astype(F32)) * (1.0 / 16.0)

    for copy in started[sent:]:
        copy.wait_send()


def body(grad_out, expert_input, expert_ids, slots, w_gate, w_up, w_down):
    saved = expert_input.transpose(0, 1, 3, 2, 4).reshape(ROWS, D)
    vmem = pl.BlockSpec(memory_space=pltpu.VMEM)
    hbm = pl.BlockSpec(memory_space=pl.ANY)
    dma = pltpu.SemaphoreType.DMA
    piece = (2, ROWS, H)
    shapes = (((1, TOK, FEAT), BF16), ((1, 256, FB), F32), ((1, 256, FB), F32))
    operands = [
        pltpu.with_memory_space_constraint(operand, pltpu.HBM)
        for operand in (expert_ids, slots, grad_out, saved, w_gate, w_up, w_down)
    ]
    return pl.pallas_call(
        kernel,
        out_shape=tuple(pltpu.VMEM(shape, dtype) for shape, dtype in shapes),
        in_specs=[hbm] * 7,
        out_specs=(vmem, vmem, vmem),
        scratch_shapes=[
            pltpu.VMEM((1, TOK), jnp.int32),
            pltpu.VMEM((1, TOK), jnp.int32),
            pltpu.VMEM((SETS, 2, TOK, H), BF16),
            pltpu.VMEM((2 * RING, ROWS, H), BF16),
            pltpu.VMEM((D, FB), BF16),
            pltpu.VMEM((D, FB), BF16),
            pltpu.VMEM((FB, D), BF16),
            pltpu.VMEM((SETS, RING, MAIN, PACK), BF16),
            pltpu.VMEM((SETS, RING, MAIN, PACK), BF16),
            pltpu.VMEM((RING,) + piece, BF16),
            pltpu.VMEM((RING,) + piece, BF16),
            pltpu.VMEM((RING,) + piece, BF16),
            pltpu.VMEM((RING,) + piece, BF16),
            pltpu.VMEM((4,) + piece, BF16),
            pltpu.VMEM((4,) + piece, BF16),
            pltpu.VMEM((RING, MAIN, PACK), BF16),
            pltpu.VMEM((RING, MAIN, PACK), BF16),
            pltpu.VMEM((2, 256, FB), BF16),
            pltpu.VMEM((2, 256, FB), BF16),
            pltpu.VMEM((2, 2, 256, FB), F32),
            dma((6,)),
            dma((SETS, 2)),
            dma((2 * RING,)),
            dma((SETS, RING)),
            dma((SETS, RING)),
            dma((RING, 2)),
            dma((RING, 2)),
            dma((RING, 3)),
            dma((RING, 3)),
            dma((2, 4, 2)),
            dma((2, 4, 2)),
            dma((2, 4, 2)),
            dma((2, 4, 2)),
            dma((2, 4, 2)),
            dma((2, 4, 2)),
            dma((RING,)),
            dma((RING,)),
            dma((2,)),
            dma((2,)),
        ],
        compiler_params=pltpu.CompilerParams(
            collective_id=0, has_side_effects=True, vmem_limit_bytes=40 * 1024 * 1024
        ),
        name="expert_backward",
    )(*operands)


def solution(mesh):
    return jax.shard_map(
        body,
        mesh=mesh,
        in_specs=(
            P("dp", "ctx", None),
            P("ctx", "dp", None, None, None),
            P("dp", "ctx"),
            P("dp", "ctx"),
            P("ctx", None, "tp"),
            P("ctx", None, "tp"),
            P("ctx", "tp", None),
        ),
        out_specs=(P("dp", "ctx", "tp"), P("ctx", "dp", "tp"), P("ctx", "dp", "tp")),
        check_vma=False,
    )
```

```python
import jax
import jax.numpy as jnp
from jax import lax
from jax.experimental import pallas as pl
from jax.experimental.pallas import tpu as pltpu
from jax.sharding import PartitionSpec as P

MESH = pl.DeviceIdType.MESH
BF16 = jnp.bfloat16
F32 = jnp.float32

RING = 8
CAP = 19
ROWS = RING * CAP
MAIN = 16
TOK = 128
D = 4096
FEAT = D // RING
H = FEAT // 2
FB = 256
PACK = FEAT + 128
SETS = 2
SHARED = (4,)


def mm(a, b, ca, cb):
    return lax.dot_general(a, b, (((ca,), (cb,)), ((), ())), preferred_element_type=F32)


def iota(shape, dim):
    return lax.broadcasted_iota(jnp.int32, shape, dim)


def onehot(mask):
    return jnp.where(mask, 1.0, 0.0).astype(BF16)


def kernel(
    ids_hbm, slots_hbm, tok_hbm, x_hbm, wg_hbm, wu_hbm, wd_hbm,
    gi_out, gg_out, gu_out,
    ids, slots, tok, x, wg, wu, wd, route_out, route_in, routed, xt, pa, part, from_left, from_right, back_out, back_in, w_out, w_in, acc,
    load_sem, tok_sem, xload_sem,
    route_ss, route_rs, xt_ss, xt_rs, share_ss, share_rs, tp_ss, tp_rs, dp_ss, dp_rs, rs_ss, rs_rs, back_ss, back_rs, w_ss, w_rs,
):
    e, t, d = lax.axis_index("ctx"), lax.axis_index("tp"), lax.axis_index("dp")
    y, a = d // 2, d % 2

    def ctx(s):
        return {"ctx": (e + s) % RING}

    def tp(s):
        return {"tp": (t + s + RING) % RING}

    def dpy(s):
        return {"dp": ((y + s + RING) % RING) * 2 + a}

    over = {"tp": (t + 2 - 4 * (t % 4 // 2) + RING) % RING}
    twin = {"dp": y * 2 + 1 - a}
    started = []

    def send(src, dst, ss, rs, dev):
        copy = pltpu.make_async_remote_copy(
            src_ref=src, dst_ref=dst, send_sem=ss, recv_sem=rs, device_id=dev, device_id_type=MESH
        )
        copy.start()
        started.append(copy)
        return copy

    load_ids = pltpu.make_async_copy(ids_hbm, ids, load_sem.at[4])
    load_slots = pltpu.make_async_copy(slots_hbm, slots, load_sem.at[5])
    load_ids.start()
    load_slots.start()
    load_tok = []
    for r, c in ((0, 0), (0, 1), (1, 0), (1, 1))[:2 * SETS]:
        first = (t + 4 * r) % RING * 2 + c
        load_tok.append(
            pltpu.make_async_copy(
                tok_hbm.at[0, :, pl.ds(pl.multiple_of(first * H, H), H)], tok.at[r, c], tok_sem.at[r, c]
            )
        )
        load_tok[-1].start()
    barrier = pltpu.get_barrier_semaphore()
    peers = [ctx(s) for s in range(1, RING)] + [tp(1), tp(-1)] + [dpy(s) for s in range(1, RING)] + [over, twin]
    for peer in peers:
        pl.semaphore_signal(barrier, inc=1, device_id=peer, device_id_type=MESH)

    load_x = [
        pltpu.make_async_copy(x_hbm.at[:, pl.ds(j * H, H)], x.at[j], xload_sem.at[j]) for j in range(2 * RING)
    ]
    for copy in load_x:
        copy.start()
    load_wg = pltpu.make_async_copy(wg_hbm.at[0], wg, load_sem.at[1])
    load_wu = pltpu.make_async_copy(wu_hbm.at[0], wu, load_sem.at[2])
    load_wd = pltpu.make_async_copy(wd_hbm.at[0], wd, load_sem.at[3])
    load_wg.start()
    load_wu.start()
    load_wd.start()

    rows = iota((TOK, TOK), 0)
    cols = iota((TOK, TOK), 1)
    main_map = onehot(cols == (rows % RING) * MAIN + rows // RING)
    erow = iota((3 * RING, TOK), 0)
    ecol = iota((3 * RING, TOK), 1)
    fold_map = [onehot(ecol == (erow % RING) * MAIN + 4 * (erow // RING) + q) for q in range(4)]

    load_ids.wait()
    load_slots.wait()
    expert, slot = ids[...], slots[...]
    main_row = jnp.where(slot < MAIN, expert * MAIN + slot, -1)
    fold_row = jnp.where(slot < MAIN, -8, expert * MAIN + 4 * (slot - MAIN))
    to_main = onehot(rows == main_row)
    to_fold = [onehot(rows == fold_row + q) for q in range(4)]
    def pack(r):
        load_tok[2 * r].wait()
        load_tok[2 * r + 1].wait()
        halves = [tok[r, c] for c in range(2)]
        for c in range(2):
            route_out[r, :, :, c * H:c * H + H] = mm(to_main, halves[c], 1, 0).astype(BF16).reshape(RING, MAIN, H)
        folded = mm(to_fold[0], halves[0][:, :128], 1, 0)
        for q in range(1, 4):
            folded = folded + mm(to_fold[q], halves[q // 2][:, (q % 2) * 128:(q % 2) * 128 + 128], 1, 0)
        route_out[r, :, :, FEAT:] = folded.astype(BF16).reshape(RING, MAIN, 128)
        route_in[r, e] = route_out[r, e]

    def route_set(r):
        return [
            send(
                route_out.at[r, (e + s) % RING], route_in.at[r, e], route_ss.at[r, s], route_rs.at[r, s], ctx(s)
            )
            for s in range(1, RING)
        ]

    def unpack(r, places):
        for copy in route[r]:
            copy.wait_recv()
        main_in = route_in[r, :, :, :FEAT].reshape(TOK, FEAT)
        fold_in = route_in[r, :, :, FEAT:].reshape(TOK, 128)
        main_part = mm(main_map, main_in, 1, 0).astype(BF16)
        fold_part = [mm(m, fold_in, 1, 0).astype(BF16) for m in fold_map]
        for c, (s, h) in enumerate(places):
            routed[s, h, :TOK, :] = main_part[:, c * H:c * H + H]
            routed[s, h, TOK:, :128] = fold_part[2 * c]
            routed[s, h, TOK:, 128:] = fold_part[2 * c + 1]

    for r in range(SETS):
        pack(r)
    pl.semaphore_wait(barrier, len(peers))
    route = [route_set(0)]

    for copy in load_x:
        copy.wait()
    quarter = t % 4
    lanes = pl.ds(pl.multiple_of(quarter % 2 * 128, 128), 128)
    quarters, xts, shares = {}, {}, {}
    for s in SHARED:
        quarters[s] = send(
            x.at[((y + s) % RING) * 2 + quarter // 2, :, lanes], xt.at[s, quarter // 2, :, lanes],
            xt_ss.at[s, 0], xt_rs.at[s, 0], dpy(s),
        )
    for s in (1, 7, 2, 6, 3, 5, 4):
        for h in range(2):
            if s not in SHARED:
                xts[s, h] = send(
                    x.at[((y + s) % RING) * 2 + h], xt.at[s, h], xt_ss.at[s, h], xt_rs.at[s, h], dpy(s)
                )
    for h in range(2):
        xt[0, h] = x[y * 2 + h]

    def share():
        for s in SHARED:
            quarters[s].wait_recv()
            piece = xt.at[s, quarter // 2, :, lanes]
            shares[s] = [
                send(piece, piece, share_ss.at[s, n], share_rs.at[s, n], peer)
                for n, peer in enumerate((tp(1), tp(-1), over))
            ]

    def saved_arrived(s):
        if s in SHARED:
            for copy in shares[s]:
                copy.wait_recv()
        elif s:
            for h in range(2):
                xts[s, h].wait_recv()

    unpack(0, ((0, 0), (0, 1)))

    def ring_send(buf, ss, rs, k, h, peer, sign):
        src, dst = (k - 1, k) if sign > 0 else ((RING + 1 - k) % RING, RING - k)
        way = 0 if sign > 0 else 1
        return send(buf.at[src, h], buf.at[dst, h], ss.at[way, k - 1, h], rs.at[way, k - 1, h], peer(sign))

    def ring_begin(buf, ss, rs, peer):
        flight = {}
        for h in range(2):
            for sign in (1, -1):
                flight[sign, 1, h] = ring_send(buf, ss, rs, 1, h, peer, sign)
        return flight

    def ring_step(flight, buf, ss, rs, peer, k, h, part_):
        for sign in (1, -1):
            flight[sign, k, h].wait_recv()
            if k < 3 or (part_ and h == (0 if sign > 0 else 1)):
                flight[sign, k + 1, h] = ring_send(buf, ss, rs, k + 1, h, peer, sign)

    def ring_end(flight):
        flight[1, 4, 0].wait_recv()
        flight[-1, 4, 1].wait_recv()

    flight = ring_begin(routed, tp_ss, tp_rs, tp)
    for r in range(1, SETS):
        route.append(route_set(r))

    load_wg.wait()
    load_wu.wait()
    gate = mm(x[0], wg[:H, :], 1, 0)
    upward = mm(x[0], wu[:H, :], 1, 0)
    for j in range(1, 2 * RING):
        gate = gate + mm(x[j], wg[j * H:j * H + H, :], 1, 0)
        upward = upward + mm(x[j], wu[j * H:j * H + H, :], 1, 0)
    sig = 1.0 / (1.0 + jnp.exp(-gate))
    up_factor = gate * sig
    gate_factor = upward * sig * (1.0 + gate * (1.0 - sig))

    load_wd.wait()

    def hidden_term(s, h):
        first = ((t - s + RING) % RING) * FEAT + h * H
        return mm(routed[s, h], wd[:, pl.ds(pl.multiple_of(first, H), H)], 1, 1)

    grad_hidden = hidden_term(0, 0) + hidden_term(0, 1)
    for k in range(1, 4):
        for h in range(2):
            ring_step(flight, routed, tp_ss, tp_rs, tp, k, h, SETS == 1)
            grad_hidden = grad_hidden + hidden_term(k, h) + hidden_term(RING - k, h)
        if k == 2 and SETS > 1:
            share()
            unpack(1, ((4, 0), (4, 1)))
            grad_hidden = grad_hidden + hidden_term(4, 0) + hidden_term(4, 1)
    if SETS == 1:
        ring_end(flight)
        grad_hidden = grad_hidden + hidden_term(4, 0) + hidden_term(4, 1)

    grad_gate_pre = (grad_hidden * gate_factor).astype(BF16)
    grad_up_pre = (grad_hidden * up_factor).astype(BF16)
    pa[0, 0] = grad_gate_pre
    pa[0, 1] = grad_up_pre

    def partial_term(j, h):
        first = pl.ds(pl.multiple_of(((t + j) % RING) * FEAT + h * H, H), H)
        part[j, h] = (mm(grad_gate_pre, wg[first, :], 1, 1) + mm(grad_up_pre, wu[first, :], 1, 1)).astype(BF16)

    rs_flight = {}

    def sum_send(sign, k, h):
        way = 0 if sign > 0 else 1
        slot_ = k if sign > 0 else RING - k
        dst = (from_left if sign > 0 else from_right).at[k - 1, h]
        rs_flight[sign, k, h] = send(
            part.at[slot_, h], dst, rs_ss.at[way, k - 1, h], rs_rs.at[way, k - 1, h], tp(sign)
        )

    def sum_step(sign, k, h):
        rs_flight[sign, k + 1, h].wait_recv()
        slot_ = k if sign > 0 else RING - k
        arrived = (from_left if sign > 0 else from_right)[k, h]
        part[slot_, h] = (part[slot_, h].astype(F32) + arrived.astype(F32)).astype(BF16)
        sum_send(sign, k, h)

    partial_term(4, 0)
    sum_send(1, 4, 0)
    partial_term(4, 1)
    sum_send(-1, 4, 1)
    dp_flight = ring_begin(pa, dp_ss, dp_rs, dpy)
    partial_term(3, 1)
    sum_send(1, 3, 1)
    partial_term(5, 0)
    sum_send(-1, 3, 0)
    partial_term(3, 0)
    partial_term(5, 1)

    def dp_step(k, h):
        ring_step(dp_flight, pa, dp_ss, dp_rs, dpy, k, h, True)

    def weight_term(s):
        saved_arrived(s)
        for half in range(2):
            for which in range(2):
                term = mm(xt[s, half], pa[s, which], 0, 0)
                acc[half, which] = acc[half, which] + term if s else term

    sum_step(1, 3, 0)
    sum_step(-1, 3, 1)
    dp_step(1, 0)
    for j in (2, 6):
        for h in range(2):
            partial_term(j, h)
    sum_step(1, 2, 1)
    sum_step(-1, 2, 0)
    dp_step(1, 1)
    weight_term(0)
    sum_step(1, 2, 0)
    sum_step(-1, 2, 1)
    dp_step(2, 0)
    for j in (1, 7, 0):
        for h in range(2):
            partial_term(j, h)
    sum_step(1, 1, 1)
    sum_step(-1, 1, 0)
    dp_step(2, 1)
    weight_term(1)
    weight_term(7)
    sum_step(1, 1, 0)
    sum_step(-1, 1, 1)
    dp_step(3, 0)
    weight_term(2)
    weight_term(6)
    dp_step(3, 1)
    weight_term(3)
    weight_term(5)
    def prepared(src, dst, ss, rs, dev):
        return pltpu.make_async_remote_copy(
            src_ref=src, dst_ref=dst, send_sem=ss, recv_sem=rs, device_id=dev, device_id_type=MESH
        )

    sent = len(started)
    w_flight = [
        prepared(w_out.at[which], w_in.at[which], w_ss.at[which], w_rs.at[which], twin) for which in range(2)
    ]
    back = [
        prepared(back_out.at[(e + s) % RING], back_in.at[e], back_ss.at[s], back_rs.at[s], ctx(s))
        for s in range(1, RING)
    ]
    started.extend(w_flight + back)

    def send_weights():
        saved_arrived(4)
        ring_end(dp_flight)
        for which in range(2):
            w_out[which] = (acc[1 - a, which] + mm(xt[4, 1 - a], pa[4, which], 0, 0)).astype(BF16)
            w_flight[which].start()

    def send_back():
        for h in (1, 0):
            rs_flight[1, 1, h].wait_recv()
            rs_flight[-1, 1, h].wait_recv()
        slot_grad = [
            (part[0, h].astype(F32) + from_left[0, h].astype(F32) + from_right[0, h].astype(F32)).astype(BF16)
            for h in range(2)
        ]
        for h in range(2):
            main_rows = mm(main_map, slot_grad[h][:TOK, :], 0, 0).astype(BF16)
            back_out[:, :, h * H:h * H + H] = main_rows.reshape(RING, MAIN, H)
        folded = mm(fold_map[0], slot_grad[0][TOK:, :128], 0, 0)
        for q in range(1, 4):
            folded = folded + mm(fold_map[q], slot_grad[q // 2][TOK:, (q % 2) * 128:(q % 2) * 128 + 128], 0, 0)
        back_out[:, :, FEAT:] = folded.astype(BF16).reshape(RING, MAIN, 128)
        for copy in back:
            copy.start()
        back_in[e] = back_out[e]

    @pl.when(e < 2)
    def weights_first():
        send_weights()
        send_back()

    @pl.when(e >= 2)
    def back_first():
        send_back()
        send_weights()

    for copy in started[:sent]:
        copy.wait_send()
    own = [acc[a, which] + mm(xt[4, a], pa[4, which], 0, 0) for which in range(2)]

    for copy in back:
        copy.wait_recv()
    main_in = back_in[:, :, :FEAT].reshape(TOK, FEAT)
    fold_in = back_in[:, :, FEAT:].reshape(TOK, 128)
    token_rows = mm(to_main, main_in, 0, 0)
    for q in range(4):
        piece = slice(128 * q, 128 * q + 128)
        gi_out[0, :, piece] = (token_rows[:, piece] + mm(to_fold[q], fold_in, 0, 0)).astype(BF16)

    for which, out in enumerate((gg_out, gu_out)):
        w_flight[which].wait_recv()
        out[0] = (own[which] + w_in[which].astype(F32)) * (1.0 / 16.0)

    for copy in started[sent:]:
        copy.wait_send()


def body(grad_out, expert_input, expert_ids, slots, w_gate, w_up, w_down):
    saved = expert_input.transpose(0, 1, 3, 2, 4).reshape(ROWS, D)
    vmem = pl.BlockSpec(memory_space=pltpu.VMEM)
    hbm = pl.BlockSpec(memory_space=pl.ANY)
    dma = pltpu.SemaphoreType.DMA
    piece = (2, ROWS, H)
    shapes = (((1, TOK, FEAT), BF16), ((1, 256, FB), F32), ((1, 256, FB), F32))
    operands = [
        pltpu.with_memory_space_constraint(operand, pltpu.HBM)
        for operand in (expert_ids, slots, grad_out, saved, w_gate, w_up, w_down)
    ]
    return pl.pallas_call(
        kernel,
        out_shape=tuple(pltpu.VMEM(shape, dtype) for shape, dtype in shapes),
        in_specs=[hbm] * 7,
        out_specs=(vmem, vmem, vmem),
        scratch_shapes=[
            pltpu.VMEM((1, TOK), jnp.int32),
            pltpu.VMEM((1, TOK), jnp.int32),
            pltpu.VMEM((SETS, 2, TOK, H), BF16),
            pltpu.VMEM((2 * RING, ROWS, H), BF16),
            pltpu.VMEM((D, FB), BF16),
            pltpu.VMEM((D, FB), BF16),
            pltpu.VMEM((FB, D), BF16),
            pltpu.VMEM((SETS, RING, MAIN, PACK), BF16),
            pltpu.VMEM((SETS, RING, MAIN, PACK), BF16),
            pltpu.VMEM((RING,) + piece, BF16),
            pltpu.VMEM((RING,) + piece, BF16),
            pltpu.VMEM((RING,) + piece, BF16),
            pltpu.VMEM((RING,) + piece, BF16),
            pltpu.VMEM((4,) + piece, BF16),
            pltpu.VMEM((4,) + piece, BF16),
            pltpu.VMEM((RING, MAIN, PACK), BF16),
            pltpu.VMEM((RING, MAIN, PACK), BF16),
            pltpu.VMEM((2, 256, FB), BF16),
            pltpu.VMEM((2, 256, FB), BF16),
            pltpu.VMEM((2, 2, 256, FB), F32),
            dma((6,)),
            dma((SETS, 2)),
            dma((2 * RING,)),
            dma((SETS, RING)),
            dma((SETS, RING)),
            dma((RING, 2)),
            dma((RING, 2)),
            dma((RING, 3)),
            dma((RING, 3)),
            dma((2, 4, 2)),
            dma((2, 4, 2)),
            dma((2, 4, 2)),
            dma((2, 4, 2)),
            dma((2, 4, 2)),
            dma((2, 4, 2)),
            dma((RING,)),
            dma((RING,)),
            dma((2,)),
            dma((2,)),
        ],
        compiler_params=pltpu.CompilerParams(
            collective_id=0, has_side_effects=True, vmem_limit_bytes=40 * 1024 * 1024
        ),
        name="expert_backward",
    )(*operands)


def solution(mesh):
    return jax.shard_map(
        body,
        mesh=mesh,
        in_specs=(
            P("dp", "ctx", None),
            P("ctx", "dp", None, None, None),
            P("dp", "ctx"),
            P("dp", "ctx"),
            P("ctx", None, "tp"),
            P("ctx", None, "tp"),
            P("ctx", "tp", None),
        ),
        out_specs=(P("dp", "ctx", "tp"), P("ctx", "dp", "tp"), P("ctx", "dp", "tp")),
        check_vma=False,
    )
```
